512 devices in a mesh: dp: 64 (over z, x), mp: 8 (over y, core).
Axes of the slice: x: 4, y: 4, z: 16, core: 2. Of those that a mesh axis runs over, the one named last changes fastest.
Arguments:
- query_rows: bfloat16 [49152, 4096], P('dp', 'mp')
- key_rows: bfloat16 [49152, 1024], P('dp', 'mp')
- value_rows: bfloat16 [49152, 1024], P('dp', 'mp'), may hold values from -6 to 6
- grad_rows: bfloat16 [49152, 4096], P('dp', 'mp'), may hold values from -6 to 6
- doc_ids: int32 [49152], P('dp'), may hold values from 0 to 383, as said below
- leaving_group: int32 [64], P('dp'), may hold values from 0 to 1
Outputs:
- attended: bfloat16 [49152, 4096], P('dp', 'mp')
- grad_query: bfloat16 [49152, 4096], P('dp', 'mp')
- grad_key: bfloat16 [49152, 1024], P('dp', 'mp')
- grad_value: bfloat16 [49152, 1024], P('dp', 'mp')
The draws below stay inside these ranges and needn't reach their ends.
Inputs may be any that keep to these rules, and one draw needn't show every extreme that they name: `doc_ids`: in each aligned run of 384 rows the numbers start at 0 and never fall; equal numbers in a run are one document.
All inputs are finite; a program needn't handle non-finite values.
Results may differ from the reference program's by a relative error of at most 0.018.
Values may be sent and summed in bfloat16 or wider, within the bound.
No kernel may reach another device: no remote copies, remote signals or barrier semaphores. Data moves between devices by JAX's collectives and lax.ppermute only.
A program may use at most 64 MiB of HBM per device.

```python
import jax
import jax.numpy as jnp
from jax import lax

HEADS = 32
KV_HEADS = 8
HEAD_DIM = 128
BINS = 2
SLOT = 384
TOK_DEV = 768
TOKENS = 49152
N_DP = 64


def draw_query_rows(key, part):
    key = jax.random.fold_in(key, 11)
    noise = jnp.clip(jax.random.normal(key, (TOKENS, HEADS * HEAD_DIM), jnp.float32), -5.5, 5.5)
    return noise.astype(jnp.bfloat16)


def draw_key_rows(key, part):
    key = jax.random.fold_in(key, 13)
    noise = jnp.clip(jax.random.normal(key, (TOKENS, KV_HEADS * HEAD_DIM), jnp.float32), -5.5, 5.5)
    return noise.astype(jnp.bfloat16)


def draw_doc_ids(key, part):
    key = jax.random.fold_in(key, 21)
    first, second = jax.random.split(key)
    limit = jax.random.randint(first, (N_DP, 1, 1), 1, 17)
    coins = jax.random.randint(second, (N_DP, BINS, SLOT), 0, 4 * SLOT)
    flags = (coins < limit).astype(jnp.int32)
    flags = flags.at[0, 0, :].set(1)
    flags = flags.at[0, 1, :].set(0)
    flags = flags.at[:, :, 0].set(0)
    numbers = jnp.cumsum(flags, axis=-1).astype(jnp.int32)
    return numbers.reshape(TOKENS)


def touch_ends(drawn, own_key, least, largest):
    extent = drawn.shape
    spot = [jax.random.randint(jax.random.fold_in(own_key, axis), (), 0, extent[axis]) for axis in range(len(extent))]
    drawn = drawn.at[tuple(spot)].set(least)
    longest = extent.index(max(extent))
    spot[longest] = (spot[longest] + 1) % extent[longest]
    return drawn.at[tuple(spot)].set(largest)


def level_of(stream_key, shape, cuts, smallest, top_value):
    level, own = 1.0, jax.random.fold_in(stream_key, 6)
    for position, blocks in cuts:
        steps = jnp.exp(jax.random.uniform(jax.random.fold_in(own, position), (blocks,), jnp.float32, smallest / len(cuts), top_value / len(cuts)))
        level = level * jnp.repeat(steps, shape[position] // blocks).reshape([-1 if axis == position else 1 for axis in range(len(shape))])
    return level


def scatter_about(key, extent, spread, most, shards=(), held_as=jnp.bfloat16):
    values = jax.random.normal(key, extent, jnp.float32) * spread
    if len(shards) > 0:
        values = level_of(key, extent, shards, -0.22, 0.18) * values
    return jnp.clip(values, min=-most, max=most).astype(held_as)


def setup_inputs(seed: int = 0) -> dict:
    seeds = jax.random.split(jax.random.key(seed), 7)
    query_rows = draw_query_rows(jax.random.fold_in(seeds[6], 71), 0)
    key_rows = draw_key_rows(jax.random.fold_in(seeds[6], 71), 0)
    value_rows = scatter_about(seeds[2], (TOKENS, KV_HEADS * HEAD_DIM), 1.0, 6.0, ((0, 64), (1, 8)))
    grad_rows = scatter_about(seeds[3], (TOKENS, HEADS * HEAD_DIM), 1.0, 6.0, ((0, 64), (1, 8)))
    doc_ids = draw_doc_ids(jax.random.fold_in(seeds[6], 71), 0)
    leaving_group = touch_ends(jax.random.randint(seeds[5], (N_DP,), 0, BINS), jax.random.fold_in(seeds[5], 1), 0, BINS - 1).astype(jnp.int32)
    return dict(query_rows=query_rows, key_rows=key_rows, value_rows=value_rows, grad_rows=grad_rows, doc_ids=doc_ids, leaving_group=leaving_group)


def attend(queries, key_block, value_block, grad_block, doc_marks, kv_heads):
    blocks, length, _ = queries.shape
    scaling = HEAD_DIM ** -0.5
    query_mat = queries.astype(jnp.float32).reshape(blocks, length, kv_heads, -1, HEAD_DIM)
    key_mat = key_block.astype(jnp.float32).reshape(blocks, length, kv_heads, HEAD_DIM)
    value_mat = value_block.astype(jnp.float32).reshape(blocks, length, kv_heads, HEAD_DIM)
    grad_mat = grad_block.astype(jnp.float32).reshape(blocks, length, kv_heads, -1, HEAD_DIM)
    places = jnp.arange(length)
    allowed = (doc_marks[:, :, None] == doc_marks[:, None, :]) & (places[None, None, :] <= places[None, :, None])
    scores = jnp.einsum('bigqd,bjgd->bgqij', query_mat, key_mat) * scaling
    scores = jnp.where(allowed[:, None, None], scores, jnp.float32(-1e30))
    row_max = jnp.max(scores, axis=-1, keepdims=True)
    weights = jnp.exp(scores - row_max)
    probs = weights / jnp.sum(weights, axis=-1, keepdims=True)
    probs16 = probs.astype(jnp.bfloat16)
    probs_wide = probs16.astype(jnp.float32)
    attended = jnp.einsum('bgqij,bjgd->bigqd', probs_wide, value_mat).astype(jnp.bfloat16)
    dprobs = jnp.einsum('bigqd,bjgd->bgqij', grad_mat, value_mat)
    inner_sum = jnp.sum(probs * dprobs, axis=-1, keepdims=True)
    dscores = (probs * (dprobs - inner_sum)).astype(jnp.bfloat16).astype(jnp.float32)
    grad_query = (jnp.einsum('bgqij,bjgd->bigqd', dscores, key_mat) * scaling).astype(jnp.bfloat16)
    grad_key = (jnp.einsum('bgqij,bigqd->bjgd', dscores, query_mat) * scaling).astype(jnp.bfloat16)
    grad_value = jnp.einsum('bgqij,bigqd->bjgd', probs_wide, grad_mat).astype(jnp.bfloat16)
    return (attended.reshape(blocks, length, -1), grad_query.reshape(blocks, length, -1),
            grad_key.reshape(blocks, length, -1), grad_value.reshape(blocks, length, -1))


def reference(query_rows, key_rows, value_rows, grad_rows, doc_ids, leaving_group):
    def one_device(device):
        offset = (device * TOK_DEV).astype(jnp.int32)

        def slice_rows(tensor):
            return lax.dynamic_slice_in_dim(tensor, offset, TOK_DEV, 0).reshape(BINS, SLOT, -1)

        doc_marks = lax.dynamic_slice_in_dim(doc_ids, offset, TOK_DEV, 0).reshape(BINS, SLOT)
        return attend(slice_rows(query_rows), slice_rows(key_rows), slice_rows(value_rows),
                      slice_rows(grad_rows), doc_marks, KV_HEADS)

    results = lax.map(one_device, jnp.arange(N_DP).astype(jnp.int32))
    devices = jnp.arange(N_DP).astype(jnp.int32)
    partner = jnp.bitwise_xor(devices, N_DP // 2).astype(jnp.int32)
    partner_bin = leaving_group[partner]
    bin_index = jnp.arange(BINS).astype(jnp.int32)
    replace = bin_index[None, :] == leaving_group[:, None]

    def held(tensor):
        moved = tensor[partner, partner_bin]
        placed = jnp.where(replace[:, :, None, None], moved[:, None], tensor)
        return placed.reshape(TOKENS, -1)

    attended, grad_query, grad_key, grad_value = results
    return (held(attended), held(grad_query), held(grad_key), held(grad_value))
```

```python
import functools

import jax
import jax.numpy as jnp
from jax import lax
from jax.experimental import pallas as pl
from jax.experimental.pallas import tpu as pltpu
from jax.sharding import PartitionSpec as P

HEAD_DIM = 128
SLOT = 384
ROWS = 128
STEPS = SLOT // ROWS
LOG2E = 1.4426950408889634
SCALING = HEAD_DIM ** (-0.5)
MASKED = -1e30 * LOG2E


def swapped(x, axis, bit):
    return lax.ppermute(x, axis, [(i, i ^ 1 << bit) for i in range(lax.axis_size(axis))])


def pack_kernel(slot_ref, q_ref, g_ref, k_ref, v_ref, out_ref, sems):
    heads = q_ref.shape[1] // HEAD_DIM
    base = pl.multiple_of(slot_ref[0] * SLOT, SLOT)
    rows = pl.ds(base, SLOT)
    parts = [q_ref.at[rows, pl.ds(h * HEAD_DIM, HEAD_DIM)] for h in range(heads)]
    parts += [g_ref.at[rows, pl.ds(h * HEAD_DIM, HEAD_DIM)] for h in range(heads)]
    parts += [k_ref.at[rows], v_ref.at[rows]]
    copies = [
        pltpu.make_async_copy(part, out_ref.at[i], sems.at[i]) for i, part in enumerate(parts)
    ]
    for copy in copies:
        copy.start()
    for copy in copies:
        copy.wait()


def pack(slot, query, grad, key, value):
    heads = query.shape[1] // HEAD_DIM
    count = 2 * heads + 2
    return pl.pallas_call(
        pack_kernel,
        out_shape=jax.ShapeDtypeStruct((count, SLOT, HEAD_DIM), query.dtype),
        in_specs=[pl.BlockSpec(memory_space=pltpu.SMEM)]
        + [pl.BlockSpec(memory_space=pltpu.HBM)] * 4,
        out_specs=pl.BlockSpec(memory_space=pl.ANY),
        scratch_shapes=[pltpu.SemaphoreType.DMA((count,))],
        name="pack_leaving",
    )(slot, query, grad, key, value)


def attend_block(step, ids, q, g, k_ref, v_ref, kt, vt, dk_acc, dv_acc, write):
    span = SLOT
    heads = len(q)
    q_all = jnp.concatenate(q, axis=0)
    g_all = jnp.concatenate(g, axis=0)
    keys, values = k_ref[:span, :], v_ref[:span, :]
    over_rows = (((1,), (1,)), ((), ()))
    scores = lax.dot_general(keys, q_all, over_rows, preferred_element_type=jnp.float32)
    dprobs = lax.dot_general(values, g_all, over_rows, preferred_element_type=jnp.float32)
    ids_t = ids.T
    key_ids = jnp.concatenate([ids_t[:, j : j + 1] for j in range(span // ROWS)], axis=0)
    places_j = lax.broadcasted_iota(jnp.int32, (span, ROWS), 0)
    places_i = lax.broadcasted_iota(jnp.int32, (span, ROWS), 1) + step * ROWS
    allowed = (key_ids == ids[step : step + 1, :]) & (places_j <= places_i)
    allowed = jnp.concatenate([allowed] * heads, axis=1)
    scores = jnp.where(allowed, scores * (SCALING * LOG2E), MASKED)
    weights = jnp.exp2(scores - jnp.max(scores, axis=0, keepdims=True))
    probs = weights * (1.0 / jnp.sum(weights, axis=0, keepdims=True))
    inner_sum = jnp.sum(probs * dprobs, axis=0, keepdims=True)
    probs16 = probs.astype(jnp.bfloat16)
    dscores = (probs * (dprobs - inner_sum)).astype(jnp.bfloat16)
    dv = jnp.dot(probs16, g_all, preferred_element_type=jnp.float32)
    dk = jnp.dot(dscores, q_all, preferred_element_type=jnp.float32)
    if step == 0:
        dv_acc[...] = dv
        dk_acc[...] = dk
    else:
        dv_acc[...] += dv
        dk_acc[...] += dk
    out_t = jnp.dot(vt[:, :span], probs16, preferred_element_type=jnp.float32)
    dq_t = jnp.dot(kt[:, :span], dscores, preferred_element_type=jnp.float32) * SCALING
    for h in range(heads):
        cols = slice(h * ROWS, (h + 1) * ROWS)
        write(h, out_t[:, cols].T.astype(jnp.bfloat16), dq_t[:, cols].T.astype(jnp.bfloat16))


def attend_kernel(received, slot_ref, docs_ref, q_ref, g_ref, k_ref, v_ref, *rest):
    if received:
        rest = rest[4:]
    o_ref, dq_ref, dk_ref, dv_ref, kt, vt, dk_acc, dv_acc = rest
    heads = o_ref.shape[1] // HEAD_DIM

    def lanes(h):
        return slice(h * HEAD_DIM, (h + 1) * HEAD_DIM)

    if received:
        marks = docs_ref[...].astype(jnp.float32)
        ids = marks[:8] * 16.0 + marks[8:]
        k_ref, v_ref = k_ref.at[0], v_ref.at[0]
    else:
        ids = docs_ref[0]

    def write(h, out, dq):
        o_ref[:, lanes(h)] = out
        dq_ref[:, lanes(h)] = dq

    index = pl.program_id(0)

    @pl.when(index == 0)
    def _():
        kt[...] = k_ref[...].T
        vt[...] = v_ref[...].T

    for step in range(STEPS):

        @pl.when(index == step)
        def _():
            if received:
                q = [q_ref[h] for h in range(heads)]
                g = [g_ref[h] for h in range(heads)]
            else:
                q = [q_ref[:, lanes(h)] for h in range(heads)]
                g = [g_ref[:, lanes(h)] for h in range(heads)]
            attend_block(step, ids, q, g, k_ref, v_ref, kt, vt, dk_acc, dv_acc, write)

    @pl.when(index == STEPS - 1)
    def _():
        dk_ref[...] = (dk_acc[...] * SCALING).astype(jnp.bfloat16)
        dv_ref[...] = dv_acc[...].astype(jnp.bfloat16)


def attend(slot, docs, inputs, in_specs, row_count, width, kv_width, held=None):
    received = held is not None
    any_spec = pl.BlockSpec(memory_space=pl.ANY)
    wide = pl.BlockSpec((ROWS, width), lambda i, s: (s[0] * STEPS + i, 0))
    narrow = pl.BlockSpec((SLOT, kv_width), lambda i, s: (s[0], 0))
    shapes = [(row_count, width)] * 2 + [(row_count, kv_width)] * 2
    work = 12 * (width // HEAD_DIM) * SLOT * SLOT * HEAD_DIM
    return pl.pallas_call(
        functools.partial(attend_kernel, received),
        out_shape=tuple(jax.ShapeDtypeStruct(shape, jnp.bfloat16) for shape in shapes),
        grid_spec=pltpu.PrefetchScalarGridSpec(
            num_scalar_prefetch=1,
            grid=(STEPS,),
            in_specs=in_specs + ([any_spec] * 4 if received else []),
            out_specs=(wide, wide, narrow, narrow),
            scratch_shapes=[
                pltpu.VMEM((HEAD_DIM, SLOT), jnp.bfloat16),
                pltpu.VMEM((HEAD_DIM, SLOT), jnp.bfloat16),
                pltpu.VMEM((SLOT, HEAD_DIM), jnp.float32),
                pltpu.VMEM((SLOT, HEAD_DIM), jnp.float32),
            ],
        ),
        input_output_aliases={6 + i: i for i in range(4)} if received else {},
        compiler_params=pltpu.CompilerParams(vmem_limit_bytes=24 * 1024 * 1024),
        cost_estimate=pl.CostEstimate(
            flops=work, bytes_accessed=4 * 1024 * 1024, transcendentals=SLOT * SLOT * 4
        ),
        name="attend_received" if received else "attend_staying",
    )(slot, docs, *inputs, *(held if received else ()))


def body(query_rows, key_rows, value_rows, grad_rows, doc_ids, leaving_group):
    row_count, width = query_rows.shape
    kv_width = key_rows.shape[1]
    heads = width // HEAD_DIM
    group_count = row_count // SLOT
    far_bit = lax.axis_size("dp").bit_length() - 2
    staying = group_count - 1 - leaving_group

    packed = pack(leaving_group, query_rows, grad_rows, key_rows, value_rows)
    arrived = swapped(packed, "dp", far_bit)

    ids = doc_ids.reshape(group_count, STEPS, ROWS)
    leaving_ids = lax.dynamic_index_in_dim(ids, leaving_group[0], 0, keepdims=False)
    marks = jnp.concatenate(
        [
            jnp.pad(leaving_ids // 16, ((0, 8 - STEPS), (0, 0))),
            jnp.pad(leaving_ids % 16, ((0, 8 - STEPS), (0, 0))),
        ],
        axis=0,
    ).astype(jnp.bfloat16)
    arrived_marks = swapped(marks, "dp", far_bit)

    docs = jnp.pad(ids.astype(jnp.float32), ((0, 0), (0, 8 - STEPS), (0, 0)))
    wide = pl.BlockSpec((ROWS, width), lambda i, s: (s[0] * STEPS + i, 0))
    narrow = pl.BlockSpec((SLOT, kv_width), lambda i, s: (s[0], 0))
    held = attend(
        staying,
        docs,
        (query_rows, grad_rows, key_rows, value_rows),
        [pl.BlockSpec((1, 8, ROWS), lambda i, s: (s[0], 0, 0)), wide, wide, narrow, narrow],
        row_count,
        width,
        kv_width,
    )

    final = attend(
        leaving_group,
        arrived_marks,
        (arrived,) * 4,
        [
            pl.BlockSpec((16, ROWS), lambda i, s: (0, 0)),
            pl.BlockSpec((heads, ROWS, HEAD_DIM), lambda i, s: (0, i, 0)),
            pl.BlockSpec((heads, ROWS, HEAD_DIM), lambda i, s: (1, i, 0)),
            pl.BlockSpec((1, SLOT, HEAD_DIM), lambda i, s: (2 * heads, 0, 0)),
            pl.BlockSpec((1, SLOT, HEAD_DIM), lambda i, s: (2 * heads + 1, 0, 0)),
        ],
        row_count,
        width,
        kv_width,
        held=held,
    )
    return tuple(final)


def solution(mesh):
    return jax.shard_map(
        body,
        mesh=mesh,
        in_specs=(P("dp", "mp"), P("dp", "mp"), P("dp", "mp"), P("dp", "mp"), P("dp"), P("dp")),
        out_specs=(P("dp", "mp"), P("dp", "mp"), P("dp", "mp"), P("dp", "mp")),
        check_vma=False,
    )
```

```python
import functools

import jax
import jax.numpy as jnp
from jax import lax
from jax.experimental import pallas as pl
from jax.experimental.pallas import tpu as pltpu
from jax.sharding import PartitionSpec as P

HEAD_DIM = 128
SLOT = 384
ROWS = 128
STEPS = SLOT // ROWS
LOG2E = 1.4426950408889634
SCALING = HEAD_DIM ** (-0.5)
MASKED = -1e30 * LOG2E


def swapped(x, axis, bit):
    return lax.ppermute(x, axis, [(i, i ^ 1 << bit) for i in range(lax.axis_size(axis))])


def pack_kernel(slot_ref, q_ref, g_ref, k_ref, v_ref, out_ref, held, sems, out_sems):
    heads = q_ref.shape[1] // HEAD_DIM
    base = pl.multiple_of(slot_ref[0] * SLOT, SLOT)
    rows = pl.ds(base, SLOT)
    parts = [q_ref.at[rows, pl.ds(h * HEAD_DIM, HEAD_DIM)] for h in range(heads)]
    parts += [g_ref.at[rows, pl.ds(h * HEAD_DIM, HEAD_DIM)] for h in range(heads)]
    parts += [k_ref.at[rows], v_ref.at[rows]]
    loads = [
        pltpu.make_async_copy(part, held.at[i], sems.at[i]) for i, part in enumerate(parts)
    ]
    stores = [
        pltpu.make_async_copy(held.at[i], out_ref.at[i], out_sems.at[i]) for i in range(len(parts))
    ]
    for load in loads:
        load.start()
    for load, store in zip(loads, stores):
        load.wait()
        store.start()
    for store in stores:
        store.wait()


def pack(slot, query, grad, key, value):
    heads = query.shape[1] // HEAD_DIM
    count = 2 * heads + 2
    return pl.pallas_call(
        pack_kernel,
        out_shape=jax.ShapeDtypeStruct((count, SLOT, HEAD_DIM), query.dtype),
        in_specs=[pl.BlockSpec(memory_space=pltpu.SMEM)]
        + [pl.BlockSpec(memory_space=pltpu.HBM)] * 4,
        out_specs=pl.BlockSpec(memory_space=pl.ANY),
        scratch_shapes=[
            pltpu.VMEM((count, SLOT, HEAD_DIM), query.dtype),
            pltpu.SemaphoreType.DMA((count,)),
            pltpu.SemaphoreType.DMA((count,)),
        ],
        name="pack_leaving",
    )(slot, query, grad, key, value)


def attend_block(step, ids, q, g, k_ref, v_ref, kt, vt, dk_acc, dv_acc, write):
    span = SLOT
    heads = len(q)
    q_all = jnp.concatenate(q, axis=0)
    g_all = jnp.concatenate(g, axis=0)
    keys, values = k_ref[:span, :], v_ref[:span, :]
    over_rows = (((1,), (1,)), ((), ()))
    scores = lax.dot_general(keys, q_all, over_rows, preferred_element_type=jnp.float32)
    dprobs = lax.dot_general(values, g_all, over_rows, preferred_element_type=jnp.float32)
    ids_t = ids.T
    key_ids = jnp.concatenate([ids_t[:, j : j + 1] for j in range(span // ROWS)], axis=0)
    places_j = lax.broadcasted_iota(jnp.int32, (span, ROWS), 0)
    places_i = lax.broadcasted_iota(jnp.int32, (span, ROWS), 1) + step * ROWS
    allowed = (key_ids == ids[step : step + 1, :]) & (places_j <= places_i)
    allowed = jnp.concatenate([allowed] * heads, axis=1)
    scores = jnp.where(allowed, scores * (SCALING * LOG2E), MASKED)
    weights = jnp.exp2(scores - jnp.max(scores, axis=0, keepdims=True))
    probs = weights * (1.0 / jnp.sum(weights, axis=0, keepdims=True))
    inner_sum = jnp.sum(probs * dprobs, axis=0, keepdims=True)
    probs16 = probs.astype(jnp.bfloat16)
    dscores = (probs * (dprobs - inner_sum)).astype(jnp.bfloat16)
    dv = jnp.dot(probs16, g_all, preferred_element_type=jnp.float32)
    dk = jnp.dot(dscores, q_all, preferred_element_type=jnp.float32)
    if step == 0:
        dv_acc[...] = dv
        dk_acc[...] = dk
    else:
        dv_acc[...] += dv
        dk_acc[...] += dk
    out_t = jnp.dot(vt[:, :span], probs16, preferred_element_type=jnp.float32)
    dq_t = jnp.dot(kt[:, :span], dscores, preferred_element_type=jnp.float32) * SCALING
    for h in range(heads):
        cols = slice(h * ROWS, (h + 1) * ROWS)
        write(h, out_t[:, cols].T.astype(jnp.bfloat16), dq_t[:, cols].T.astype(jnp.bfloat16))


def attend_kernel(received, slot_ref, docs_ref, q_ref, g_ref, k_ref, v_ref, *rest):
    if received:
        rest = rest[4:]
    o_ref, dq_ref, dk_ref, dv_ref, kt, vt, dk_acc, dv_acc = rest
    heads = o_ref.shape[1] // HEAD_DIM

    def lanes(h):
        return slice(h * HEAD_DIM, (h + 1) * HEAD_DIM)

    if received:
        marks = docs_ref[...].astype(jnp.float32)
        ids = marks[:8] * 16.0 + marks[8:]
        k_ref, v_ref = k_ref.at[0], v_ref.at[0]
    else:
        ids = docs_ref[0]

    def write(h, out, dq):
        o_ref[:, lanes(h)] = out
        dq_ref[:, lanes(h)] = dq

    index = pl.program_id(0)

    @pl.when(index == 0)
    def _():
        kt[...] = k_ref[...].T
        vt[...] = v_ref[...].T

    for step in range(STEPS):

        @pl.when(index == step)
        def _():
            if received:
                q = [q_ref[h] for h in range(heads)]
                g = [g_ref[h] for h in range(heads)]
            else:
                q = [q_ref[:, lanes(h)] for h in range(heads)]
                g = [g_ref[:, lanes(h)] for h in range(heads)]
            attend_block(step, ids, q, g, k_ref, v_ref, kt, vt, dk_acc, dv_acc, write)

    @pl.when(index == STEPS - 1)
    def _():
        dk_ref[...] = (dk_acc[...] * SCALING).astype(jnp.bfloat16)
        dv_ref[...] = dv_acc[...].astype(jnp.bfloat16)


def attend(slot, docs, inputs, in_specs, row_count, width, kv_width, held=None):
    received = held is not None
    any_spec = pl.BlockSpec(memory_space=pl.ANY)
    wide = pl.BlockSpec((ROWS, width), lambda i, s: (s[0] * STEPS + i, 0))
    narrow = pl.BlockSpec((SLOT, kv_width), lambda i, s: (s[0], 0))
    shapes = [(row_count, width)] * 2 + [(row_count, kv_width)] * 2
    work = 12 * (width // HEAD_DIM) * SLOT * SLOT * HEAD_DIM
    return pl.pallas_call(
        functools.partial(attend_kernel, received),
        out_shape=tuple(jax.ShapeDtypeStruct(shape, jnp.bfloat16) for shape in shapes),
        grid_spec=pltpu.PrefetchScalarGridSpec(
            num_scalar_prefetch=1,
            grid=(STEPS,),
            in_specs=in_specs + ([any_spec] * 4 if received else []),
            out_specs=(wide, wide, narrow, narrow),
            scratch_shapes=[
                pltpu.VMEM((HEAD_DIM, SLOT), jnp.bfloat16),
                pltpu.VMEM((HEAD_DIM, SLOT), jnp.bfloat16),
                pltpu.VMEM((SLOT, HEAD_DIM), jnp.float32),
                pltpu.VMEM((SLOT, HEAD_DIM), jnp.float32),
            ],
        ),
        input_output_aliases={6 + i: i for i in range(4)} if received else {},
        compiler_params=pltpu.CompilerParams(vmem_limit_bytes=24 * 1024 * 1024),
        cost_estimate=pl.CostEstimate(
            flops=work, bytes_accessed=4 * 1024 * 1024, transcendentals=SLOT * SLOT * 4
        ),
        name="attend_received" if received else "attend_staying",
    )(slot, docs, *inputs, *(held if received else ()))


def body(query_rows, key_rows, value_rows, grad_rows, doc_ids, leaving_group):
    row_count, width = query_rows.shape
    kv_width = key_rows.shape[1]
    heads = width // HEAD_DIM
    group_count = row_count // SLOT
    far_bit = lax.axis_size("dp").bit_length() - 2
    staying = group_count - 1 - leaving_group

    packed = pack(leaving_group, query_rows, grad_rows, key_rows, value_rows)
    arrived = swapped(packed, "dp", far_bit)

    ids = doc_ids.reshape(group_count, STEPS, ROWS)
    leaving_ids = lax.dynamic_index_in_dim(ids, leaving_group[0], 0, keepdims=False)
    marks = jnp.concatenate(
        [
            jnp.pad(leaving_ids // 16, ((0, 8 - STEPS), (0, 0))),
            jnp.pad(leaving_ids % 16, ((0, 8 - STEPS), (0, 0))),
        ],
        axis=0,
    ).astype(jnp.bfloat16)
    arrived_marks = swapped(marks, "dp", far_bit)

    docs = jnp.pad(ids.astype(jnp.float32), ((0, 0), (0, 8 - STEPS), (0, 0)))
    wide = pl.BlockSpec((ROWS, width), lambda i, s: (s[0] * STEPS + i, 0))
    narrow = pl.BlockSpec((SLOT, kv_width), lambda i, s: (s[0], 0))
    held = attend(
        staying,
        docs,
        (query_rows, grad_rows, key_rows, value_rows),
        [pl.BlockSpec((1, 8, ROWS), lambda i, s: (s[0], 0, 0)), wide, wide, narrow, narrow],
        row_count,
        width,
        kv_width,
    )

    final = attend(
        leaving_group,
        arrived_marks,
        (arrived,) * 4,
        [
            pl.BlockSpec((16, ROWS), lambda i, s: (0, 0)),
            pl.BlockSpec((heads, ROWS, HEAD_DIM), lambda i, s: (0, i, 0)),
            pl.BlockSpec((heads, ROWS, HEAD_DIM), lambda i, s: (1, i, 0)),
            pl.BlockSpec((1, SLOT, HEAD_DIM), lambda i, s: (2 * heads, 0, 0)),
            pl.BlockSpec((1, SLOT, HEAD_DIM), lambda i, s: (2 * heads + 1, 0, 0)),
        ],
        row_count,
        width,
        kv_width,
        held=held,
    )
    return tuple(final)


def solution(mesh):
    return jax.shard_map(
        body,
        mesh=mesh,
        in_specs=(P("dp", "mp"), P("dp", "mp"), P("dp", "mp"), P("dp", "mp"), P("dp"), P("dp")),
        out_specs=(P("dp", "mp"), P("dp", "mp"), P("dp", "mp"), P("dp", "mp")),
        check_vma=False,
    )
```

```python
import functools

import jax
import jax.numpy as jnp
from jax import lax
from jax.experimental import pallas as pl
from jax.experimental.pallas import tpu as pltpu
from jax.sharding import PartitionSpec as P

HEAD_DIM = 128
SLOT = 384
LANES = 128
RUNS = SLOT // LANES
LOG2E = 1.4426950408889634
SCALING = HEAD_DIM ** (-0.5)
MASKED = -1e30 * LOG2E
OVER_LANES = (((1,), (1,)), ((), ()))
HBM = pl.BlockSpec(memory_space=pltpu.HBM)


def swapped(x, axis, bit):
    return lax.ppermute(x, axis, [(i, i ^ 1 << bit) for i in range(lax.axis_size(axis))])


def pack_kernel(heads, whole, slot_ref, *refs):
    if whole:
        *inputs, ids_ref, out_ref, ids, sems = refs
        ids_copy = pltpu.make_async_copy(ids_ref, ids, sems.at[sems.shape[0] - 1])
        ids_copy.start()
    else:
        *inputs, out_ref, sems = refs
    rows = pl.ds(pl.multiple_of(slot_ref[0] * SLOT, SLOT), SLOT)
    parts = [
        ref.at[rows, pl.ds(h * HEAD_DIM, HEAD_DIM)] for ref in inputs[:2] for h in heads
    ]
    parts += [ref.at[rows] for ref in inputs[2:]]
    copies = [
        pltpu.make_async_copy(part, out_ref.at[pl.ds(i * SLOT, SLOT)], sems.at[i])
        for i, part in enumerate(parts)
    ]
    for copy in copies:
        copy.start()
    if whole:
        ids_copy.wait()
        lines = [
            ids[j * LANES : (j + 1) * LANES].reshape(1, LANES) for j in range(ids.shape[0] // LANES)
        ]
        here = jnp.concatenate(lines[:RUNS], axis=0)
        for group in range(1, len(lines) // RUNS):
            other = jnp.concatenate(lines[group * RUNS : (group + 1) * RUNS], axis=0)
            here = jnp.where(slot_ref[0] == group, other, here)
        blank = jnp.zeros((8 - RUNS, LANES), jnp.int32)
        marks = jnp.concatenate([here >> 4, blank, here & 15, blank], axis=0)
        out_ref[len(parts) * SLOT :, :] = marks.astype(jnp.float32).astype(out_ref.dtype)
    for copy in copies:
        copy.wait()


def pack(slot, heads, query, grad, pair=(), doc_ids=None):
    whole = doc_ids is not None
    count = 2 * len(heads) + len(pair)
    inputs = (query, grad, *pair) + ((doc_ids,) if whole else ())
    inputs = [pltpu.with_memory_space_constraint(x, pltpu.HBM) for x in inputs]
    packed = jax.ShapeDtypeStruct((count * SLOT + 16 * whole, HEAD_DIM), query.dtype)
    scratch = [pltpu.VMEM(doc_ids.shape, jnp.int32)] if whole else []
    return pl.pallas_call(
        functools.partial(pack_kernel, heads, whole),
        out_shape=packed,
        in_specs=[pl.BlockSpec(memory_space=pltpu.SMEM)] + [HBM] * len(inputs),
        out_specs=pl.BlockSpec(memory_space=pltpu.VMEM),
        scratch_shapes=scratch + [pltpu.SemaphoreType.DMA((count + whole,))],
        compiler_params=pltpu.CompilerParams(vmem_limit_bytes=4 * 1024 * 1024),
        name="pack_" + "_".join(str(h) for h in heads),
    )(slot, *inputs)


def attend_head(ids, q, g, keys, values, keys_t, values_t):
    scores = lax.dot_general(keys, q, OVER_LANES, preferred_element_type=jnp.float32)
    dprobs = lax.dot_general(values, g, OVER_LANES, preferred_element_type=jnp.float32)
    ids_t = ids.T
    key_ids = jnp.concatenate([ids_t[:, j : j + 1] for j in range(RUNS)], axis=0)
    row_ids = jnp.concatenate([ids[j : j + 1, :] for j in range(RUNS)], axis=1)
    key_places = lax.broadcasted_iota(jnp.int32, (SLOT, SLOT), 0)
    row_places = lax.broadcasted_iota(jnp.int32, (SLOT, SLOT), 1)
    allowed = (key_ids == row_ids) & (key_places <= row_places)
    scores = jnp.where(allowed, scores * (SCALING * LOG2E), MASKED)
    weights = jnp.exp2(scores - jnp.max(scores, axis=0, keepdims=True))
    probs = weights * (1.0 / jnp.sum(weights, axis=0, keepdims=True))
    inner_sum = jnp.sum(probs * dprobs, axis=0, keepdims=True)
    probs16 = probs.astype(jnp.bfloat16)
    dscores = (probs * (dprobs - inner_sum)).astype(jnp.bfloat16)
    dv = jnp.dot(probs16, g, preferred_element_type=jnp.float32)
    dk = jnp.dot(dscores, q, preferred_element_type=jnp.float32)
    out_t = jnp.dot(values_t, probs16, preferred_element_type=jnp.float32)
    dq_t = jnp.dot(keys_t, dscores, preferred_element_type=jnp.float32) * SCALING
    return out_t.T.astype(jnp.bfloat16), dq_t.T.astype(jnp.bfloat16), dk, dv


def attend_kernel(count, first, last, held, slot_ref, marks_ref, q_ref, g_ref, k_ref, v_ref, *rest):
    if not first:
        dk_in, dv_in, *rest = rest
    o_ref, dq_ref, dk_ref, dv_ref, keys_t, values_t, dk_sum, dv_sum = rest[held:]
    index = pl.program_id(0)

    @pl.when(index == 0)
    def _():
        keys_t[...] = k_ref[...].T
        values_t[...] = v_ref[...].T
        dk_sum[...] = jnp.zeros_like(dk_sum) if first else dk_in[...]
        dv_sum[...] = jnp.zeros_like(dv_sum) if first else dv_in[...]

    marks = marks_ref[...].astype(jnp.float32)
    ids = marks[:8] * 16.0 + marks[8:]
    out, dq, dk, dv = attend_head(
        ids, q_ref[...], g_ref[...], k_ref[...], v_ref[...], keys_t[...], values_t[...]
    )
    o_ref[...] = out
    dq_ref[...] = dq
    dk_sum[...] += dk
    dv_sum[...] += dv

    @pl.when(index == count - 1)
    def _():
        if last:
            dk_ref[...] = (dk_sum[...] * SCALING).astype(jnp.bfloat16)
            dv_ref[...] = dv_sum[...].astype(jnp.bfloat16)
        else:
            dk_ref[...] = dk_sum[...]
            dv_ref[...] = dv_sum[...]


def attend(slot, heads, inputs, places, row_count, width, partial=None, held=(), last=True):
    def block(place, rows=SLOT):
        return pl.BlockSpec((rows, HEAD_DIM), place)

    first = partial is None
    wide = block(lambda h, s: (s[0], h + heads[0]))
    whole = block(lambda h, s: (0, 0))
    narrow = block(lambda h, s: (s[0], 0)) if last else whole
    in_specs = [block(places[0], 16)] + [block(place) for place in places[1:]]
    in_specs += [whole, whole] * (not first) + [pl.BlockSpec(memory_space=pl.ANY)] * len(held)
    sum_shape = jax.ShapeDtypeStruct((SLOT, HEAD_DIM), jnp.float32)
    wide_shape = jax.ShapeDtypeStruct((row_count, width), jnp.bfloat16)
    narrow_shape = jax.ShapeDtypeStruct((row_count, HEAD_DIM), jnp.bfloat16)
    begin = 1 + len(inputs) + 2 * (not first)
    return pl.pallas_call(
        functools.partial(attend_kernel, len(heads), first, last, len(held)),
        out_shape=(wide_shape, wide_shape) + ((narrow_shape,) * 2 if last else (sum_shape,) * 2),
        grid_spec=pltpu.PrefetchScalarGridSpec(
            num_scalar_prefetch=1,
            grid=(len(heads),),
            in_specs=in_specs,
            out_specs=(wide, wide, narrow, narrow),
            scratch_shapes=[pltpu.VMEM((HEAD_DIM, SLOT), jnp.bfloat16)] * 2
            + [pltpu.VMEM((SLOT, HEAD_DIM), jnp.float32)] * 2,
        ),
        input_output_aliases={begin + i: i for i in range(len(held))},
        compiler_params=pltpu.CompilerParams(vmem_limit_bytes=16 * 1024 * 1024),
        cost_estimate=pl.CostEstimate(
            flops=12 * len(heads) * SLOT * SLOT * HEAD_DIM,
            bytes_accessed=(4 * len(heads) + 4) * SLOT * HEAD_DIM * 2,
            transcendentals=SLOT * SLOT * len(heads),
        ),
        name="attend_" + "_".join(str(h) for h in heads),
    )(slot, *inputs, *(() if first else partial), *held)


def body(query_rows, key_rows, value_rows, grad_rows, doc_ids, leaving_group):
    row_count, width = query_rows.shape
    heads = tuple(range(width // HEAD_DIM))
    early, late = heads[:-1], heads[-1:]
    group_count = row_count // SLOT
    far_bit = lax.axis_size("dp").bit_length() - 2

    most = pack(leaving_group, early, query_rows, grad_rows, (key_rows, value_rows), doc_ids)
    most, query_rows, grad_rows = lax.optimization_barrier((most, query_rows, grad_rows))
    most = swapped(most, "dp", far_bit)
    rest = pack(leaving_group, late, query_rows, grad_rows)
    rest = swapped(rest, "dp", far_bit)

    ids = jnp.pad(doc_ids.reshape(group_count, RUNS, LANES), ((0, 0), (0, 8 - RUNS), (0, 0)))
    marks = jnp.concatenate([ids // 16, ids % 16], axis=1).astype(jnp.bfloat16)
    staying = group_count - 1 - leaving_group

    held = attend(
        staying,
        heads,
        (marks.reshape(group_count * 16, LANES), query_rows, grad_rows, key_rows, value_rows),
        (
            lambda h, s: (s[0], 0),
            lambda h, s: (s[0], h),
            lambda h, s: (s[0], h),
            lambda h, s: (s[0], 0),
            lambda h, s: (s[0], 0),
        ),
        row_count,
        width,
    )

    pair_at = 2 * len(early)
    marks_at = (pair_at + 2) * (SLOT // 16)

    def marks_place(h, s):
        return (marks_at, 0)

    pair_places = (lambda h, s: (pair_at, 0), lambda h, s: (pair_at + 1, 0))
    out, dq, *partial = attend(
        leaving_group,
        early,
        (most, most, most, most, most),
        (
            marks_place,
            lambda h, s: (h, 0),
            lambda h, s: (h + len(early), 0),
            *pair_places,
        ),
        row_count,
        width,
        held=held[:2],
        last=False,
    )
    return tuple(
        attend(
            leaving_group,
            late,
            (most, rest, rest, most, most),
            (
                marks_place,
                lambda h, s: (0, 0),
                lambda h, s: (1, 0),
                *pair_places,
            ),
            row_count,
            width,
            partial=partial,
            held=(out, dq, *held[2:]),
        )
    )


def solution(mesh):
    return jax.shard_map(
        body,
        mesh=mesh,
        in_specs=(P("dp", "mp"), P("dp", "mp"), P("dp", "mp"), P("dp", "mp"), P("dp"), P("dp")),
        out_specs=(P("dp", "mp"), P("dp", "mp"), P("dp", "mp"), P("dp", "mp")),
        check_vma=False,
    )
```

```python
import functools

import jax
import jax.numpy as jnp
from jax import lax
from jax.experimental import pallas as pl
from jax.experimental.pallas import tpu as pltpu
from jax.sharding import PartitionSpec as P

HEAD_DIM = 128
SLOT = 384
LANES = 128
RUNS = SLOT // LANES
LOG2E = 1.4426950408889634
SCALING = HEAD_DIM ** (-0.5)
MASKED = -1e30 * LOG2E
OVER_LANES = (((1,), (1,)), ((), ()))
RING = 16
YIELDING = (5, 7)
HBM = pl.BlockSpec(memory_space=pltpu.HBM)


def swapped(x, axis, bit):
    return lax.ppermute(x, axis, [(i, i ^ 1 << bit) for i in range(lax.axis_size(axis))])


def pack_kernel(heads, whole, slot_ref, *refs):
    if whole:
        *inputs, ids_ref, out_ref, ids, sems = refs
        ids_copy = pltpu.make_async_copy(ids_ref, ids, sems.at[sems.shape[0] - 1])
        ids_copy.start()
    else:
        *inputs, out_ref, sems = refs
    rows = pl.ds(pl.multiple_of(slot_ref[0] * SLOT, SLOT), SLOT)
    parts = [
        ref.at[rows, pl.ds(h * HEAD_DIM, HEAD_DIM)] for ref in inputs[:2] for h in heads
    ]
    parts += [ref.at[rows] for ref in inputs[2:]]
    copies = [
        pltpu.make_async_copy(part, out_ref.at[pl.ds(i * SLOT, SLOT)], sems.at[i])
        for i, part in enumerate(parts)
    ]
    if whole:
        place = lax.axis_index("dp") * RING // lax.axis_size("dp")
        yields = functools.reduce(jnp.logical_or, [place == z for z in YIELDING])
        half = len(copies) // 2
        for copy in copies[:half]:
            copy.start()

        @pl.when(yields)
        def _():
            for copy in copies[:half]:
                copy.wait()

        for copy in copies[half:]:
            copy.start()
        ids_copy.wait()
        lines = [
            ids[j * LANES : (j + 1) * LANES].reshape(1, LANES) for j in range(ids.shape[0] // LANES)
        ]
        here = jnp.concatenate(lines[:RUNS], axis=0)
        for group in range(1, len(lines) // RUNS):
            other = jnp.concatenate(lines[group * RUNS : (group + 1) * RUNS], axis=0)
            here = jnp.where(slot_ref[0] == group, other, here)
        blank = jnp.zeros((8 - RUNS, LANES), jnp.int32)
        marks = jnp.concatenate([here >> 4, blank, here & 15, blank], axis=0)
        out_ref[len(parts) * SLOT :, :] = marks.astype(jnp.float32).astype(out_ref.dtype)

        @pl.when(jnp.logical_not(yields))
        def _():
            for copy in copies[:half]:
                copy.wait()

        for copy in copies[half:]:
            copy.wait()
    else:
        for copy in copies:
            copy.start()
        for copy in copies:
            copy.wait()


def pack(slot, heads, query, grad, pair=(), doc_ids=None):
    whole = doc_ids is not None
    count = 2 * len(heads) + len(pair)
    inputs = (query, grad, *pair) + ((doc_ids,) if whole else ())
    inputs = [pltpu.with_memory_space_constraint(x, pltpu.HBM) for x in inputs]
    packed = jax.ShapeDtypeStruct((count * SLOT + 16 * whole, HEAD_DIM), query.dtype)
    scratch = [pltpu.VMEM(doc_ids.shape, jnp.int32)] if whole else []
    return pl.pallas_call(
        functools.partial(pack_kernel, heads, whole),
        out_shape=packed,
        in_specs=[pl.BlockSpec(memory_space=pltpu.SMEM)] + [HBM] * len(inputs),
        out_specs=pl.BlockSpec(memory_space=pltpu.VMEM),
        scratch_shapes=scratch + [pltpu.SemaphoreType.DMA((count + whole,))],
        compiler_params=pltpu.CompilerParams(vmem_limit_bytes=4 * 1024 * 1024),
        name="pack_" + "_".join(str(h) for h in heads),
    )(slot, *inputs)


def attend_head(ids, q, g, keys, values, keys_t, values_t):
    scores = lax.dot_general(keys, q, OVER_LANES, preferred_element_type=jnp.float32)
    dprobs = lax.dot_general(values, g, OVER_LANES, preferred_element_type=jnp.float32)
    ids_t = ids.T
    key_ids = jnp.concatenate([ids_t[:, j : j + 1] for j in range(RUNS)], axis=0)
    row_ids = jnp.concatenate([ids[j : j + 1, :] for j in range(RUNS)], axis=1)
    key_places = lax.broadcasted_iota(jnp.int32, (SLOT, SLOT), 0)
    row_places = lax.broadcasted_iota(jnp.int32, (SLOT, SLOT), 1)
    allowed = (key_ids == row_ids) & (key_places <= row_places)
    scores = jnp.where(allowed, scores * (SCALING * LOG2E), MASKED)
    weights = jnp.exp2(scores - jnp.max(scores, axis=0, keepdims=True))
    probs = weights * (1.0 / jnp.sum(weights, axis=0, keepdims=True))
    inner_sum = jnp.sum(probs * dprobs, axis=0, keepdims=True)
    probs16 = probs.astype(jnp.bfloat16)
    dscores = (probs * (dprobs - inner_sum)).astype(jnp.bfloat16)
    dv = jnp.dot(probs16, g, preferred_element_type=jnp.float32)
    dk = jnp.dot(dscores, q, preferred_element_type=jnp.float32)
    out_t = jnp.dot(values_t, probs16, preferred_element_type=jnp.float32)
    dq_t = jnp.dot(keys_t, dscores, preferred_element_type=jnp.float32) * SCALING
    return out_t.T.astype(jnp.bfloat16), dq_t.T.astype(jnp.bfloat16), dk, dv


def attend_kernel(count, first, last, held, slot_ref, marks_ref, q_ref, g_ref, k_ref, v_ref, *rest):
    if not first:
        dk_in, dv_in, *rest = rest
    o_ref, dq_ref, dk_ref, dv_ref, keys_t, values_t, dk_sum, dv_sum = rest[held:]
    index = pl.program_id(0)

    @pl.when(index == 0)
    def _():
        keys_t[...] = k_ref[...].T
        values_t[...] = v_ref[...].T
        dk_sum[...] = jnp.zeros_like(dk_sum) if first else dk_in[...]
        dv_sum[...] = jnp.zeros_like(dv_sum) if first else dv_in[...]

    marks = marks_ref[...].astype(jnp.float32)
    ids = marks[:8] * 16.0 + marks[8:]
    out, dq, dk, dv = attend_head(
        ids, q_ref[...], g_ref[...], k_ref[...], v_ref[...], keys_t[...], values_t[...]
    )
    o_ref[...] = out
    dq_ref[...] = dq
    dk_sum[...] += dk
    dv_sum[...] += dv

    @pl.when(index == count - 1)
    def _():
        if last:
            dk_ref[...] = (dk_sum[...] * SCALING).astype(jnp.bfloat16)
            dv_ref[...] = dv_sum[...].astype(jnp.bfloat16)
        else:
            dk_ref[...] = dk_sum[...]
            dv_ref[...] = dv_sum[...]


def attend(slot, heads, inputs, places, row_count, width, partial=None, held=(), last=True):
    def block(place, rows=SLOT):
        return pl.BlockSpec((rows, HEAD_DIM), place)

    first = partial is None
    wide = block(lambda h, s: (s[0], h + heads[0]))
    whole = block(lambda h, s: (0, 0))
    narrow = block(lambda h, s: (s[0], 0)) if last else whole
    in_specs = [block(places[0], 16)] + [block(place) for place in places[1:]]
    in_specs += [whole, whole] * (not first) + [pl.BlockSpec(memory_space=pl.ANY)] * len(held)
    sum_shape = jax.ShapeDtypeStruct((SLOT, HEAD_DIM), jnp.float32)
    wide_shape = jax.ShapeDtypeStruct((row_count, width), jnp.bfloat16)
    narrow_shape = jax.ShapeDtypeStruct((row_count, HEAD_DIM), jnp.bfloat16)
    begin = 1 + len(inputs) + 2 * (not first)
    return pl.pallas_call(
        functools.partial(attend_kernel, len(heads), first, last, len(held)),
        out_shape=(wide_shape, wide_shape) + ((narrow_shape,) * 2 if last else (sum_shape,) * 2),
        grid_spec=pltpu.PrefetchScalarGridSpec(
            num_scalar_prefetch=1,
            grid=(len(heads),),
            in_specs=in_specs,
            out_specs=(wide, wide, narrow, narrow),
            scratch_shapes=[pltpu.VMEM((HEAD_DIM, SLOT), jnp.bfloat16)] * 2
            + [pltpu.VMEM((SLOT, HEAD_DIM), jnp.float32)] * 2,
        ),
        input_output_aliases={begin + i: i for i in range(len(held))},
        compiler_params=pltpu.CompilerParams(vmem_limit_bytes=16 * 1024 * 1024),
        cost_estimate=pl.CostEstimate(
            flops=12 * len(heads) * SLOT * SLOT * HEAD_DIM,
            bytes_accessed=(4 * len(heads) + 4) * SLOT * HEAD_DIM * 2,
            transcendentals=SLOT * SLOT * len(heads),
        ),
        name="attend_" + "_".join(str(h) for h in heads),
    )(slot, *inputs, *(() if first else partial), *held)


def body(query_rows, key_rows, value_rows, grad_rows, doc_ids, leaving_group):
    row_count, width = query_rows.shape
    heads = tuple(range(width // HEAD_DIM))
    early, late = heads[:-1], heads[-1:]
    group_count = row_count // SLOT
    far_bit = lax.axis_size("dp").bit_length() - 2

    most = pack(leaving_group, early, query_rows, grad_rows, (key_rows, value_rows), doc_ids)
    most, query_rows, grad_rows = lax.optimization_barrier((most, query_rows, grad_rows))
    most = swapped(most, "dp", far_bit)
    rest = pack(leaving_group, late, query_rows, grad_rows)
    rest = swapped(rest, "dp", far_bit)

    ids = jnp.pad(doc_ids.reshape(group_count, RUNS, LANES), ((0, 0), (0, 8 - RUNS), (0, 0)))
    marks = jnp.concatenate([ids // 16, ids % 16], axis=1).astype(jnp.bfloat16)
    staying = group_count - 1 - leaving_group

    held = attend(
        staying,
        heads,
        (marks.reshape(group_count * 16, LANES), query_rows, grad_rows, key_rows, value_rows),
        (
            lambda h, s: (s[0], 0),
            lambda h, s: (s[0], h),
            lambda h, s: (s[0], h),
            lambda h, s: (s[0], 0),
            lambda h, s: (s[0], 0),
        ),
        row_count,
        width,
    )

    pair_at = 2 * len(early)
    marks_at = (pair_at + 2) * (SLOT // 16)

    def marks_place(h, s):
        return (marks_at, 0)

    pair_places = (lambda h, s: (pair_at, 0), lambda h, s: (pair_at + 1, 0))
    out, dq, *partial = attend(
        leaving_group,
        early,
        (most, most, most, most, most),
        (
            marks_place,
            lambda h, s: (h, 0),
            lambda h, s: (h + len(early), 0),
            *pair_places,
        ),
        row_count,
        width,
        held=held[:2],
        last=False,
    )
    return tuple(
        attend(
            leaving_group,
            late,
            (most, rest, rest, most, most),
            (
                marks_place,
                lambda h, s: (0, 0),
                lambda h, s: (1, 0),
                *pair_places,
            ),
            row_count,
            width,
            partial=partial,
            held=(out, dq, *held[2:]),
        )
    )


def solution(mesh):
    return jax.shard_map(
        body,
        mesh=mesh,
        in_specs=(P("dp", "mp"), P("dp", "mp"), P("dp", "mp"), P("dp", "mp"), P("dp"), P("dp")),
        out_specs=(P("dp", "mp"), P("dp", "mp"), P("dp", "mp"), P("dp", "mp")),
        check_vma=False,
    )
```

```python
import functools

import jax
import jax.numpy as jnp
from jax import lax
from jax.experimental import pallas as pl
from jax.experimental.pallas import tpu as pltpu
from jax.sharding import PartitionSpec as P

HEAD_DIM = 128
SLOT = 384
LANES = 128
RUNS = SLOT // LANES
LOG2E = 1.4426950408889634
SCALING = HEAD_DIM ** (-0.5)
MASKED = -1e30 * LOG2E
OVER_LANES = (((1,), (1,)), ((), ()))
RING = 16
YIELDING = (5, 7)
HBM = pl.BlockSpec(memory_space=pltpu.HBM)


def swapped(x, axis, bit):
    return lax.ppermute(x, axis, [(i, i ^ 1 << bit) for i in range(lax.axis_size(axis))])


def in_hbm(arrays):
    return [pltpu.with_memory_space_constraint(x, pltpu.HBM) for x in arrays]


def pack_kernel(heads, whole, slot_ref, *refs):
    if whole:
        *inputs, ids_ref, out_ref, ids, sems = refs
        ids_copy = pltpu.make_async_copy(ids_ref, ids, sems.at[sems.shape[0] - 1])
        ids_copy.start()
    else:
        *inputs, out_ref, sems = refs
    rows = pl.ds(pl.multiple_of(slot_ref[0] * SLOT, SLOT), SLOT)
    parts = [
        ref.at[rows, pl.ds(h * HEAD_DIM, HEAD_DIM)] for ref in inputs[:2] for h in heads
    ]
    parts += [ref.at[rows] for ref in inputs[2:]]
    copies = [
        pltpu.make_async_copy(part, out_ref.at[pl.ds(i * SLOT, SLOT)], sems.at[i])
        for i, part in enumerate(parts)
    ]
    if whole:
        place = lax.axis_index("dp") * RING // lax.axis_size("dp")
        yields = functools.reduce(jnp.logical_or, [place == z for z in YIELDING])
        half = len(copies) // 2
        for copy in copies[:half]:
            copy.start()

        @pl.when(yields)
        def _():
            for copy in copies[:half]:
                copy.wait()

        for copy in copies[half:]:
            copy.start()
        ids_copy.wait()
        lines = [
            ids[j * LANES : (j + 1) * LANES].reshape(1, LANES) for j in range(ids.shape[0] // LANES)
        ]
        here = jnp.concatenate(lines[:RUNS], axis=0)
        for group in range(1, len(lines) // RUNS):
            other = jnp.concatenate(lines[group * RUNS : (group + 1) * RUNS], axis=0)
            here = jnp.where(slot_ref[0] == group, other, here)
        blank = jnp.zeros((8 - RUNS, LANES), jnp.int32)
        marks = jnp.concatenate([here >> 4, blank, here & 15, blank], axis=0)
        out_ref[len(parts) * SLOT :, :] = marks.astype(jnp.float32).astype(out_ref.dtype)

        @pl.when(jnp.logical_not(yields))
        def _():
            for copy in copies[:half]:
                copy.wait()

        for copy in copies[half:]:
            copy.wait()
    else:
        for copy in copies:
            copy.start()
        for copy in copies:
            copy.wait()


def pack(slot, heads, query, grad, pair=(), doc_ids=None):
    whole = doc_ids is not None
    count = 2 * len(heads) + len(pair)
    inputs = (query, grad, *pair) + ((doc_ids,) if whole else ())
    inputs = in_hbm(inputs)
    packed = jax.ShapeDtypeStruct((count * SLOT + 16 * whole, HEAD_DIM), query.dtype)
    scratch = [pltpu.VMEM(doc_ids.shape, jnp.int32)] if whole else []
    return pl.pallas_call(
        functools.partial(pack_kernel, heads, whole),
        out_shape=packed,
        in_specs=[pl.BlockSpec(memory_space=pltpu.SMEM)] + [HBM] * len(inputs),
        out_specs=pl.BlockSpec(memory_space=pltpu.VMEM),
        scratch_shapes=scratch + [pltpu.SemaphoreType.DMA((count + whole,))],
        compiler_params=pltpu.CompilerParams(vmem_limit_bytes=4 * 1024 * 1024),
        name="pack_" + "_".join(str(h) for h in heads),
    )(slot, *inputs)


def attend_weights(ids, q, g, keys, values):
    scores = lax.dot_general(keys, q, OVER_LANES, preferred_element_type=jnp.float32)
    dprobs = lax.dot_general(values, g, OVER_LANES, preferred_element_type=jnp.float32)
    ids_t = ids.T
    key_ids = jnp.concatenate([ids_t[:, j : j + 1] for j in range(RUNS)], axis=0)
    row_ids = jnp.concatenate([ids[j : j + 1, :] for j in range(RUNS)], axis=1)
    key_places = lax.broadcasted_iota(jnp.int32, (SLOT, SLOT), 0)
    row_places = lax.broadcasted_iota(jnp.int32, (SLOT, SLOT), 1)
    allowed = (key_ids == row_ids) & (key_places <= row_places)
    scores = jnp.where(allowed, scores * (SCALING * LOG2E), MASKED)
    weights = jnp.exp2(scores - jnp.max(scores, axis=0, keepdims=True))
    probs = weights * (1.0 / jnp.sum(weights, axis=0, keepdims=True))
    inner_sum = jnp.sum(probs * dprobs, axis=0, keepdims=True)
    probs16 = probs.astype(jnp.bfloat16)
    return probs16, (probs * (dprobs - inner_sum)).astype(jnp.bfloat16)


def attend_head(ids, q, g, keys, values, keys_t, values_t):
    probs16, dscores = attend_weights(ids, q, g, keys, values)
    dv = jnp.dot(probs16, g, preferred_element_type=jnp.float32)
    dk = jnp.dot(dscores, q, preferred_element_type=jnp.float32)
    out_t = jnp.dot(values_t, probs16, preferred_element_type=jnp.float32)
    dq_t = jnp.dot(keys_t, dscores, preferred_element_type=jnp.float32) * SCALING
    return out_t.T.astype(jnp.bfloat16), dq_t.T.astype(jnp.bfloat16), dk, dv


def numbers(marks):
    marks = marks.astype(jnp.float32)
    return marks[:8] * 16.0 + marks[8:]


def attend_kernel(count, whole, held, slot_ref, marks_ref, q_ref, g_ref, k_ref, v_ref, *rest):
    o_ref, dq_ref, dk_ref, dv_ref, keys_t, values_t, dk_sum, dv_sum = rest[held:]
    index = pl.program_id(0)

    @pl.when(index == 0)
    def _():
        keys_t[...] = k_ref[...].T
        values_t[...] = v_ref[...].T
        dk_sum[...] = jnp.zeros_like(dk_sum)
        dv_sum[...] = jnp.zeros_like(dv_sum)

    ids = numbers(marks_ref[...])
    out, dq, dk, dv = attend_head(
        ids, q_ref[...], g_ref[...], k_ref[...], v_ref[...], keys_t[...], values_t[...]
    )
    o_ref[...] = out
    dq_ref[...] = dq
    dk_sum[...] += dk
    dv_sum[...] += dv

    @pl.when(index == count - 1)
    def _():
        if whole:
            dk_ref[...] = (dk_sum[...] * SCALING).astype(jnp.bfloat16)
            dv_ref[...] = dv_sum[...].astype(jnp.bfloat16)
        else:
            dk_ref[...] = dk_sum[...]
            dv_ref[...] = dv_sum[...]


def work(count):
    return pl.CostEstimate(
        flops=12 * count * SLOT * SLOT * HEAD_DIM,
        bytes_accessed=(4 * count + 4) * SLOT * HEAD_DIM * 2,
        transcendentals=SLOT * SLOT * count,
    )


def attend(slot, heads, inputs, places, row_count, width, held=()):
    def block(place, rows=SLOT):
        return pl.BlockSpec((rows, HEAD_DIM), place)

    whole = len(held) == 0
    wide = block(lambda h, s: (s[0], h))
    narrow = block(lambda h, s: (s[0], 0) if whole else (0, 0))
    flat = pl.BlockSpec((HEAD_DIM, SLOT), lambda h, s: (0, 0))
    in_specs = [block(places[0], 16)] + [block(place) for place in places[1:]]
    in_specs += [pl.BlockSpec(memory_space=pl.ANY)] * len(held)
    wide_shape = jax.ShapeDtypeStruct((row_count, width), jnp.bfloat16)
    narrow_shape = jax.ShapeDtypeStruct((row_count, HEAD_DIM), jnp.bfloat16)
    sum_shape = jax.ShapeDtypeStruct((SLOT, HEAD_DIM), jnp.float32)
    flat_shape = jax.ShapeDtypeStruct((HEAD_DIM, SLOT), jnp.bfloat16)
    return pl.pallas_call(
        functools.partial(attend_kernel, len(heads), whole, len(held)),
        out_shape=(wide_shape,) * 2
        + ((narrow_shape,) * 2 if whole else (sum_shape,) * 2 + (flat_shape,) * 2),
        grid_spec=pltpu.PrefetchScalarGridSpec(
            num_scalar_prefetch=1,
            grid=(len(heads),),
            in_specs=in_specs,
            out_specs=(wide, wide, narrow, narrow) + (flat,) * 2 * (not whole),
            scratch_shapes=[pltpu.VMEM((HEAD_DIM, SLOT), jnp.bfloat16)] * 2 * whole
            + [pltpu.VMEM((SLOT, HEAD_DIM), jnp.float32)] * 2,
        ),
        input_output_aliases={1 + len(inputs) + i: i for i in range(len(held))},
        compiler_params=pltpu.CompilerParams(vmem_limit_bytes=16 * 1024 * 1024),
        cost_estimate=work(len(heads)),
        name="attend_" + "_".join(str(h) for h in heads),
    )(slot, *inputs, *held)


def finish_kernel(head, blocks, slot_ref, most, rest, dk_in, dv_in, keys_t, values_t, *refs):
    o_ref, dq_ref, dk_ref, dv_ref, made, sems = refs[4:]
    rows = pl.ds(pl.multiple_of(slot_ref[0] * SLOT, SLOT), SLOT)
    cols = pl.ds(head * HEAD_DIM, HEAD_DIM)
    copies = [
        pltpu.make_async_copy(made.at[i], place, sems.at[i])
        for i, place in enumerate(
            (o_ref.at[rows, cols], dq_ref.at[rows, cols], dk_ref.at[rows], dv_ref.at[rows])
        )
    ]

    def give(i, value):
        made[i] = value.astype(jnp.bfloat16)
        copies[i].start()

    q, g = rest[:SLOT, :], rest[SLOT:, :]
    keys = most[blocks * SLOT : (blocks + 1) * SLOT, :]
    values = most[(blocks + 1) * SLOT : (blocks + 2) * SLOT, :]
    ids = numbers(most[(blocks + 2) * SLOT :, :])
    probs16, dscores = attend_weights(ids, q, g, keys, values)
    give(3, dv_in[...] + jnp.dot(probs16, g, preferred_element_type=jnp.float32))
    give(0, jnp.dot(values_t[...], probs16, preferred_element_type=jnp.float32).T)
    dk = dk_in[...] + jnp.dot(dscores, q, preferred_element_type=jnp.float32)
    give(2, dk * SCALING)
    give(1, (jnp.dot(keys_t[...], dscores, preferred_element_type=jnp.float32) * SCALING).T)
    for copy in copies:
        copy.wait()


def finish(slot, head, most, rest, sums, held):
    vmem = pl.BlockSpec(memory_space=pltpu.VMEM)
    anywhere = pl.BlockSpec(memory_space=pl.ANY)
    blocks = most.shape[0] // SLOT - 2
    begin = 3 + len(sums)
    return pl.pallas_call(
        functools.partial(finish_kernel, head, blocks),
        out_shape=tuple(jax.ShapeDtypeStruct(x.shape, x.dtype) for x in held),
        in_specs=[pl.BlockSpec(memory_space=pltpu.SMEM)] + [vmem] * (begin - 1) + [anywhere] * 4,
        out_specs=(anywhere,) * 4,
        scratch_shapes=[
            pltpu.VMEM((4, SLOT, HEAD_DIM), jnp.bfloat16),
            pltpu.SemaphoreType.DMA((4,)),
        ],
        input_output_aliases={begin + i: i for i in range(4)},
        compiler_params=pltpu.CompilerParams(vmem_limit_bytes=16 * 1024 * 1024),
        cost_estimate=work(1),
        name="finish",
    )(slot, most, rest, *sums, *held)


def body(query_rows, key_rows, value_rows, grad_rows, doc_ids, leaving_group):
    row_count, width = query_rows.shape
    heads = tuple(range(width // HEAD_DIM))
    early, late = heads[:-1], heads[-1:]
    group_count = row_count // SLOT
    far_bit = lax.axis_size("dp").bit_length() - 2

    most = pack(leaving_group, early, query_rows, grad_rows, (key_rows, value_rows), doc_ids)
    most, query_rows, grad_rows = lax.optimization_barrier((most, query_rows, grad_rows))
    most = swapped(most, "dp", far_bit)
    rest = pack(leaving_group, late, query_rows, grad_rows)
    rest = swapped(rest, "dp", far_bit)

    ids = jnp.pad(doc_ids.reshape(group_count, RUNS, LANES), ((0, 0), (0, 8 - RUNS), (0, 0)))
    marks = jnp.concatenate([ids // 16, ids % 16], axis=1).astype(jnp.bfloat16)
    staying = group_count - 1 - leaving_group

    held = attend(
        staying,
        heads,
        (
            marks.reshape(group_count * 16, LANES),
            *in_hbm((query_rows, grad_rows, key_rows, value_rows)),
        ),
        (
            lambda h, s: (s[0], 0),
            lambda h, s: (s[0], h),
            lambda h, s: (s[0], h),
            lambda h, s: (s[0], 0),
            lambda h, s: (s[0], 0),
        ),
        row_count,
        width,
    )

    pair_at = 2 * len(early)
    marks_at = (pair_at + 2) * (SLOT // 16)

    def marks_place(h, s):
        return (marks_at, 0)

    pair_places = (lambda h, s: (pair_at, 0), lambda h, s: (pair_at + 1, 0))
    out, dq, *sums = attend(
        leaving_group,
        early,
        (most, most, most, most, most),
        (
            marks_place,
            lambda h, s: (h, 0),
            lambda h, s: (h + len(early), 0),
            *pair_places,
        ),
        row_count,
        width,
        held=held[:2],
    )
    return tuple(finish(leaving_group, late[0], most, rest, sums, (out, dq, *held[2:])))


def solution(mesh):
    return jax.shard_map(
        body,
        mesh=mesh,
        in_specs=(P("dp", "mp"), P("dp", "mp"), P("dp", "mp"), P("dp", "mp"), P("dp"), P("dp")),
        out_specs=(P("dp", "mp"), P("dp", "mp"), P("dp", "mp"), P("dp", "mp")),
        check_vma=False,
    )
```

```python
import functools

import jax
import jax.numpy as jnp
from jax import lax
from jax.experimental import pallas as pl
from jax.experimental.pallas import tpu as pltpu
from jax.sharding import PartitionSpec as P

HEAD_DIM = 128
SLOT = 384
LANES = 128
RUNS = SLOT // LANES
LOG2E = 1.4426950408889634
SCALING = HEAD_DIM ** (-0.5)
MASKED = -1e30 * LOG2E
OVER_LANES = (((1,), (1,)), ((), ()))
RING = 16
YIELDING = (5, 7, 11, 13)
HBM = pl.BlockSpec(memory_space=pltpu.HBM)


def swapped(x, axis, bit):
    return lax.ppermute(x, axis, [(i, i ^ 1 << bit) for i in range(lax.axis_size(axis))])


def in_hbm(arrays):
    return [pltpu.with_memory_space_constraint(x, pltpu.HBM) for x in arrays]


def pack_kernel(heads, whole, slot_ref, *refs):
    if whole:
        *inputs, ids_ref, out_ref, ids, sems = refs
        ids_copy = pltpu.make_async_copy(ids_ref, ids, sems.at[sems.shape[0] - 1])
        ids_copy.start()
    else:
        *inputs, out_ref, sems = refs
    rows = pl.ds(pl.multiple_of(slot_ref[0] * SLOT, SLOT), SLOT)
    parts = [
        ref.at[rows, pl.ds(h * HEAD_DIM, HEAD_DIM)] for ref in inputs[:2] for h in heads
    ]
    parts += [ref.at[rows] for ref in inputs[2:]]
    copies = [
        pltpu.make_async_copy(part, out_ref.at[pl.ds(i * SLOT, SLOT)], sems.at[i])
        for i, part in enumerate(parts)
    ]
    if whole:
        place = lax.axis_index("dp") * RING // lax.axis_size("dp")
        yields = functools.reduce(jnp.logical_or, [place == z for z in YIELDING])
        half = len(copies) // 2
        for copy in copies[:half]:
            copy.start()

        @pl.when(yields)
        def _():
            for copy in copies[:half]:
                copy.wait()

        for copy in copies[half:]:
            copy.start()
        ids_copy.wait()
        lines = [
            ids[j * LANES : (j + 1) * LANES].reshape(1, LANES) for j in range(ids.shape[0] // LANES)
        ]
        here = jnp.concatenate(lines[:RUNS], axis=0)
        for group in range(1, len(lines) // RUNS):
            other = jnp.concatenate(lines[group * RUNS : (group + 1) * RUNS], axis=0)
            here = jnp.where(slot_ref[0] == group, other, here)
        blank = jnp.zeros((8 - RUNS, LANES), jnp.int32)
        marks = jnp.concatenate([here >> 4, blank, here & 15, blank], axis=0)
        out_ref[len(parts) * SLOT :, :] = marks.astype(jnp.float32).astype(out_ref.dtype)

        @pl.when(jnp.logical_not(yields))
        def _():
            for copy in copies[:half]:
                copy.wait()

        for copy in copies[half:]:
            copy.wait()
    else:
        for copy in copies:
            copy.start()
        for copy in copies:
            copy.wait()


def pack(slot, heads, query, grad, pair=(), doc_ids=None):
    whole = doc_ids is not None
    count = 2 * len(heads) + len(pair)
    inputs = (query, grad, *pair) + ((doc_ids,) if whole else ())
    inputs = in_hbm(inputs)
    packed = jax.ShapeDtypeStruct((count * SLOT + 16 * whole, HEAD_DIM), query.dtype)
    scratch = [pltpu.VMEM(doc_ids.shape, jnp.int32)] if whole else []
    return pl.pallas_call(
        functools.partial(pack_kernel, heads, whole),
        out_shape=packed,
        in_specs=[pl.BlockSpec(memory_space=pltpu.SMEM)] + [HBM] * len(inputs),
        out_specs=pl.BlockSpec(memory_space=pltpu.VMEM),
        scratch_shapes=scratch + [pltpu.SemaphoreType.DMA((count + whole,))],
        compiler_params=pltpu.CompilerParams(vmem_limit_bytes=4 * 1024 * 1024),
        name="pack_" + "_".join(str(h) for h in heads),
    )(slot, *inputs)


def attend_weights(ids, q, g, keys, values):
    scores = lax.dot_general(keys, q, OVER_LANES, preferred_element_type=jnp.float32)
    dprobs = lax.dot_general(values, g, OVER_LANES, preferred_element_type=jnp.float32)
    ids_t = ids.T
    key_ids = jnp.concatenate([ids_t[:, j : j + 1] for j in range(RUNS)], axis=0)
    row_ids = jnp.concatenate([ids[j : j + 1, :] for j in range(RUNS)], axis=1)
    key_places = lax.broadcasted_iota(jnp.int32, (SLOT, SLOT), 0)
    row_places = lax.broadcasted_iota(jnp.int32, (SLOT, SLOT), 1)
    allowed = (key_ids == row_ids) & (key_places <= row_places)
    scores = jnp.where(allowed, scores * (SCALING * LOG2E), MASKED)
    weights = jnp.exp2(scores - jnp.max(scores, axis=0, keepdims=True))
    probs = weights * (1.0 / jnp.sum(weights, axis=0, keepdims=True))
    inner_sum = jnp.sum(probs * dprobs, axis=0, keepdims=True)
    probs16 = probs.astype(jnp.bfloat16)
    return probs16, (probs * (dprobs - inner_sum)).astype(jnp.bfloat16)


def attend_head(ids, q, g, keys, values, keys_t, values_t):
    probs16, dscores = attend_weights(ids, q, g, keys, values)
    dv = jnp.dot(probs16, g, preferred_element_type=jnp.float32)
    dk = jnp.dot(dscores, q, preferred_element_type=jnp.float32)
    out_t = jnp.dot(values_t, probs16, preferred_element_type=jnp.float32)
    dq_t = jnp.dot(keys_t, dscores, preferred_element_type=jnp.float32) * SCALING
    return out_t.T.astype(jnp.bfloat16), dq_t.T.astype(jnp.bfloat16), dk, dv


def numbers(marks):
    marks = marks.astype(jnp.float32)
    return marks[:8] * 16.0 + marks[8:]


def attend_kernel(count, whole, held, slot_ref, marks_ref, q_ref, g_ref, k_ref, v_ref, *rest):
    o_ref, dq_ref, dk_ref, dv_ref, keys_t, values_t, dk_sum, dv_sum = rest[held:]
    index = pl.program_id(0)

    @pl.when(index == 0)
    def _():
        keys_t[...] = k_ref[...].T
        values_t[...] = v_ref[...].T
        dk_sum[...] = jnp.zeros_like(dk_sum)
        dv_sum[...] = jnp.zeros_like(dv_sum)

    ids = numbers(marks_ref[...])
    out, dq, dk, dv = attend_head(
        ids, q_ref[...], g_ref[...], k_ref[...], v_ref[...], keys_t[...], values_t[...]
    )
    o_ref[...] = out
    dq_ref[...] = dq
    dk_sum[...] += dk
    dv_sum[...] += dv

    @pl.when(index == count - 1)
    def _():
        if whole:
            dk_ref[...] = (dk_sum[...] * SCALING).astype(jnp.bfloat16)
            dv_ref[...] = dv_sum[...].astype(jnp.bfloat16)
        else:
            dk_ref[...] = dk_sum[...]
            dv_ref[...] = dv_sum[...]


def work(count):
    return pl.CostEstimate(
        flops=12 * count * SLOT * SLOT * HEAD_DIM,
        bytes_accessed=(4 * count + 4) * SLOT * HEAD_DIM * 2,
        transcendentals=SLOT * SLOT * count,
    )


def attend(slot, heads, inputs, places, row_count, width, held=()):
    def block(place, rows=SLOT):
        return pl.BlockSpec((rows, HEAD_DIM), place)

    whole = len(held) == 0
    wide = block(lambda h, s: (s[0], h))
    narrow = block(lambda h, s: (s[0], 0) if whole else (0, 0))
    flat = pl.BlockSpec((HEAD_DIM, SLOT), lambda h, s: (0, 0))
    in_specs = [block(places[0], 16)] + [block(place) for place in places[1:]]
    in_specs += [pl.BlockSpec(memory_space=pl.ANY)] * len(held)
    wide_shape = jax.ShapeDtypeStruct((row_count, width), jnp.bfloat16)
    narrow_shape = jax.ShapeDtypeStruct((row_count, HEAD_DIM), jnp.bfloat16)
    sum_shape = jax.ShapeDtypeStruct((SLOT, HEAD_DIM), jnp.float32)
    flat_shape = jax.ShapeDtypeStruct((HEAD_DIM, SLOT), jnp.bfloat16)
    return pl.pallas_call(
        functools.partial(attend_kernel, len(heads), whole, len(held)),
        out_shape=(wide_shape,) * 2
        + ((narrow_shape,) * 2 if whole else (sum_shape,) * 2 + (flat_shape,) * 2),
        grid_spec=pltpu.PrefetchScalarGridSpec(
            num_scalar_prefetch=1,
            grid=(len(heads),),
            in_specs=in_specs,
            out_specs=(wide, wide, narrow, narrow) + (flat,) * 2 * (not whole),
            scratch_shapes=[pltpu.VMEM((HEAD_DIM, SLOT), jnp.bfloat16)] * 2 * whole
            + [pltpu.VMEM((SLOT, HEAD_DIM), jnp.float32)] * 2,
        ),
        input_output_aliases={1 + len(inputs) + i: i for i in range(len(held))},
        compiler_params=pltpu.CompilerParams(vmem_limit_bytes=16 * 1024 * 1024),
        cost_estimate=work(len(heads)),
        name="attend_" + "_".join(str(h) for h in heads),
    )(slot, *inputs, *held)


def finish_kernel(head, blocks, slot_ref, most, rest, dk_in, dv_in, keys_t, values_t, *refs):
    o_ref, dq_ref, dk_ref, dv_ref, made, sems = refs[4:]
    rows = pl.ds(pl.multiple_of(slot_ref[0] * SLOT, SLOT), SLOT)
    cols = pl.ds(head * HEAD_DIM, HEAD_DIM)
    copies = [
        pltpu.make_async_copy(made.at[i], place, sems.at[i])
        for i, place in enumerate(
            (o_ref.at[rows, cols], dq_ref.at[rows, cols], dk_ref.at[rows], dv_ref.at[rows])
        )
    ]

    def give(i, value):
        made[i] = value.astype(jnp.bfloat16)
        copies[i].start()

    q, g = rest[:SLOT, :], rest[SLOT:, :]
    keys = most[blocks * SLOT : (blocks + 1) * SLOT, :]
    values = most[(blocks + 1) * SLOT : (blocks + 2) * SLOT, :]
    ids = numbers(most[(blocks + 2) * SLOT :, :])
    probs16, dscores = attend_weights(ids, q, g, keys, values)
    give(3, dv_in[...] + jnp.dot(probs16, g, preferred_element_type=jnp.float32))
    give(0, jnp.dot(values_t[...], probs16, preferred_element_type=jnp.float32).T)
    dk = dk_in[...] + jnp.dot(dscores, q, preferred_element_type=jnp.float32)
    give(2, dk * SCALING)
    give(1, (jnp.dot(keys_t[...], dscores, preferred_element_type=jnp.float32) * SCALING).T)
    for copy in copies:
        copy.wait()


def finish(slot, head, most, rest, sums, held):
    vmem = pl.BlockSpec(memory_space=pltpu.VMEM)
    anywhere = pl.BlockSpec(memory_space=pl.ANY)
    blocks = most.shape[0] // SLOT - 2
    begin = 3 + len(sums)
    return pl.pallas_call(
        functools.partial(finish_kernel, head, blocks),
        out_shape=tuple(jax.ShapeDtypeStruct(x.shape, x.dtype) for x in held),
        in_specs=[pl.BlockSpec(memory_space=pltpu.SMEM)] + [vmem] * (begin - 1) + [anywhere] * 4,
        out_specs=(anywhere,) * 4,
        scratch_shapes=[
            pltpu.VMEM((4, SLOT, HEAD_DIM), jnp.bfloat16),
            pltpu.SemaphoreType.DMA((4,)),
        ],
        input_output_aliases={begin + i: i for i in range(4)},
        compiler_params=pltpu.CompilerParams(vmem_limit_bytes=16 * 1024 * 1024),
        cost_estimate=work(1),
        name="finish",
    )(slot, most, rest, *sums, *held)


def body(query_rows, key_rows, value_rows, grad_rows, doc_ids, leaving_group):
    row_count, width = query_rows.shape
    heads = tuple(range(width // HEAD_DIM))
    early, late = heads[:-1], heads[-1:]
    group_count = row_count // SLOT
    far_bit = lax.axis_size("dp").bit_length() - 2

    most = pack(leaving_group, early, query_rows, grad_rows, (key_rows, value_rows), doc_ids)
    most, query_rows, grad_rows = lax.optimization_barrier((most, query_rows, grad_rows))
    most = swapped(most, "dp", far_bit)
    rest = pack(leaving_group, late, query_rows, grad_rows)
    rest = swapped(rest, "dp", far_bit)

    ids = jnp.pad(doc_ids.reshape(group_count, RUNS, LANES), ((0, 0), (0, 8 - RUNS), (0, 0)))
    marks = jnp.concatenate([ids // 16, ids % 16], axis=1).astype(jnp.bfloat16)
    staying = group_count - 1 - leaving_group

    held = attend(
        staying,
        heads,
        (
            marks.reshape(group_count * 16, LANES),
            *in_hbm((query_rows, grad_rows, key_rows, value_rows)),
        ),
        (
            lambda h, s: (s[0], 0),
            lambda h, s: (s[0], h),
            lambda h, s: (s[0], h),
            lambda h, s: (s[0], 0),
            lambda h, s: (s[0], 0),
        ),
        row_count,
        width,
    )

    pair_at = 2 * len(early)
    marks_at = (pair_at + 2) * (SLOT // 16)

    def marks_place(h, s):
        return (marks_at, 0)

    pair_places = (lambda h, s: (pair_at, 0), lambda h, s: (pair_at + 1, 0))
    out, dq, *sums = attend(
        leaving_group,
        early,
        (most, most, most, most, most),
        (
            marks_place,
            lambda h, s: (h, 0),
            lambda h, s: (h + len(early), 0),
            *pair_places,
        ),
        row_count,
        width,
        held=held[:2],
    )
    return tuple(finish(leaving_group, late[0], most, rest, sums, (out, dq, *held[2:])))


def solution(mesh):
    return jax.shard_map(
        body,
        mesh=mesh,
        in_specs=(P("dp", "mp"), P("dp", "mp"), P("dp", "mp"), P("dp", "mp"), P("dp"), P("dp")),
        out_specs=(P("dp", "mp"), P("dp", "mp"), P("dp", "mp"), P("dp", "mp")),
        check_vma=False,
    )
```

```python
import functools

import jax
import jax.numpy as jnp
from jax import lax
from jax.experimental import pallas as pl
from jax.experimental.pallas import tpu as pltpu
from jax.sharding import PartitionSpec as P

HEAD_DIM = 128
SLOT = 384
LANES = 128
RUNS = SLOT // LANES
LOG2E = 1.4426950408889634
SCALING = HEAD_DIM ** (-0.5)
MASKED = -1e30 * LOG2E
OVER_LANES = (((1,), (1,)), ((), ()))
RING = 16
YIELDING = (5, 7, 11, 13)
HBM = pl.BlockSpec(memory_space=pltpu.HBM)


def swapped(x, axis, bit):
    return lax.ppermute(x, axis, [(i, i ^ 1 << bit) for i in range(lax.axis_size(axis))])


def in_hbm(arrays):
    return [pltpu.with_memory_space_constraint(x, pltpu.HBM) for x in arrays]


def pack_kernel(q_heads, g_heads, whole, slot_ref, *refs):
    if whole:
        *inputs, ids_ref, out_ref, ids, sems = refs
        ids_copy = pltpu.make_async_copy(ids_ref, ids, sems.at[sems.shape[0] - 1])
        ids_copy.start()
    else:
        *inputs, out_ref, sems = refs
    rows = pl.ds(pl.multiple_of(slot_ref[0] * SLOT, SLOT), SLOT)
    parts = [
        ref.at[rows, pl.ds(h * HEAD_DIM, HEAD_DIM)]
        for ref, heads in zip(inputs, (q_heads, g_heads))
        for h in heads
    ]
    parts += [ref.at[rows] for ref in inputs[2:]]
    copies = [
        pltpu.make_async_copy(part, out_ref.at[pl.ds(i * SLOT, SLOT)], sems.at[i])
        for i, part in enumerate(parts)
    ]
    if whole:
        place = lax.axis_index("dp") * RING // lax.axis_size("dp")
        yields = functools.reduce(jnp.logical_or, [place == z for z in YIELDING])
        half = len(copies) // 2
        for copy in copies[:half]:
            copy.start()

        @pl.when(yields)
        def _():
            for copy in copies[:half]:
                copy.wait()

        for copy in copies[half:]:
            copy.start()
        ids_copy.wait()
        lines = [
            ids[j * LANES : (j + 1) * LANES].reshape(1, LANES) for j in range(ids.shape[0] // LANES)
        ]
        here = jnp.concatenate(lines[:RUNS], axis=0)
        for group in range(1, len(lines) // RUNS):
            other = jnp.concatenate(lines[group * RUNS : (group + 1) * RUNS], axis=0)
            here = jnp.where(slot_ref[0] == group, other, here)
        blank = jnp.zeros((8 - RUNS, LANES), jnp.int32)
        marks = jnp.concatenate([here >> 4, blank, here & 15, blank], axis=0)
        out_ref[len(parts) * SLOT :, :] = marks.astype(jnp.float32).astype(out_ref.dtype)

        @pl.when(jnp.logical_not(yields))
        def _():
            for copy in copies[:half]:
                copy.wait()

        for copy in copies[half:]:
            copy.wait()
    else:
        for copy in copies:
            copy.start()
        for copy in copies:
            copy.wait()


def pack(slot, q_heads, g_heads, query, grad, pair=(), doc_ids=None):
    whole = doc_ids is not None
    count = len(q_heads) + len(g_heads) + len(pair)
    inputs = (query, grad, *pair) + ((doc_ids,) if whole else ())
    inputs = in_hbm(inputs)
    packed = jax.ShapeDtypeStruct((count * SLOT + 16 * whole, HEAD_DIM), query.dtype)
    scratch = [pltpu.VMEM(doc_ids.shape, jnp.int32)] if whole else []
    return pl.pallas_call(
        functools.partial(pack_kernel, q_heads, g_heads, whole),
        out_shape=packed,
        in_specs=[pl.BlockSpec(memory_space=pltpu.SMEM)] + [HBM] * len(inputs),
        out_specs=pl.BlockSpec(memory_space=pltpu.VMEM),
        scratch_shapes=scratch + [pltpu.SemaphoreType.DMA((count + whole,))],
        compiler_params=pltpu.CompilerParams(vmem_limit_bytes=4 * 1024 * 1024),
        name=f"pack_{count}",
    )(slot, *inputs)


def attend_probs(ids, q, keys):
    scores = lax.dot_general(keys, q, OVER_LANES, preferred_element_type=jnp.float32)
    ids_t = ids.T
    key_ids = jnp.concatenate([ids_t[:, j : j + 1] for j in range(RUNS)], axis=0)
    row_ids = jnp.concatenate([ids[j : j + 1, :] for j in range(RUNS)], axis=1)
    key_places = lax.broadcasted_iota(jnp.int32, (SLOT, SLOT), 0)
    row_places = lax.broadcasted_iota(jnp.int32, (SLOT, SLOT), 1)
    allowed = (key_ids == row_ids) & (key_places <= row_places)
    scores = jnp.where(allowed, scores * (SCALING * LOG2E), MASKED)
    weights = jnp.exp2(scores - jnp.max(scores, axis=0, keepdims=True))
    return weights * (1.0 / jnp.sum(weights, axis=0, keepdims=True))


def attend_dscores(probs, g, values):
    dprobs = lax.dot_general(values, g, OVER_LANES, preferred_element_type=jnp.float32)
    inner_sum = jnp.sum(probs * dprobs, axis=0, keepdims=True)
    return (probs * (dprobs - inner_sum)).astype(jnp.bfloat16)


def attend_head(ids, q, g, keys, values, keys_t, values_t):
    probs = attend_probs(ids, q, keys)
    probs16 = probs.astype(jnp.bfloat16)
    dscores = attend_dscores(probs, g, values)
    dv = jnp.dot(probs16, g, preferred_element_type=jnp.float32)
    dk = jnp.dot(dscores, q, preferred_element_type=jnp.float32)
    out_t = jnp.dot(values_t, probs16, preferred_element_type=jnp.float32)
    dq_t = jnp.dot(keys_t, dscores, preferred_element_type=jnp.float32) * SCALING
    return out_t.T.astype(jnp.bfloat16), dq_t.T.astype(jnp.bfloat16), dk, dv


def numbers(marks):
    marks = marks.astype(jnp.float32)
    return marks[:8] * 16.0 + marks[8:]


def attend_kernel(count, whole, held, slot_ref, marks_ref, q_ref, g_ref, k_ref, v_ref, *rest):
    o_ref, dq_ref, dk_ref, dv_ref, keys_t, values_t, dk_sum, dv_sum = rest[held:]
    index = pl.program_id(0)

    @pl.when(index == 0)
    def _():
        keys_t[...] = k_ref[...].T
        values_t[...] = v_ref[...].T
        dk_sum[...] = jnp.zeros_like(dk_sum)
        dv_sum[...] = jnp.zeros_like(dv_sum)

    ids = numbers(marks_ref[...])
    out, dq, dk, dv = attend_head(
        ids, q_ref[...], g_ref[...], k_ref[...], v_ref[...], keys_t[...], values_t[...]
    )
    o_ref[...] = out
    dq_ref[...] = dq
    dk_sum[...] += dk
    dv_sum[...] += dv

    @pl.when(index == count - 1)
    def _():
        if whole:
            dk_ref[...] = (dk_sum[...] * SCALING).astype(jnp.bfloat16)
            dv_ref[...] = dv_sum[...].astype(jnp.bfloat16)
        else:
            dk_ref[...] = dk_sum[...]
            dv_ref[...] = dv_sum[...]


def work(count):
    return pl.CostEstimate(
        flops=12 * count * SLOT * SLOT * HEAD_DIM,
        bytes_accessed=(4 * count + 4) * SLOT * HEAD_DIM * 2,
        transcendentals=SLOT * SLOT * count,
    )


def attend(slot, heads, inputs, places, row_count, width, held=()):
    def block(place, rows=SLOT):
        return pl.BlockSpec((rows, HEAD_DIM), place)

    whole = len(held) == 0
    wide = block(lambda h, s: (s[0], h))
    narrow = block(lambda h, s: (s[0], 0) if whole else (0, 0))
    flat = pl.BlockSpec((HEAD_DIM, SLOT), lambda h, s: (0, 0))
    in_specs = [block(places[0], 16)] + [block(place) for place in places[1:]]
    in_specs += [pl.BlockSpec(memory_space=pl.ANY)] * len(held)
    wide_shape = jax.ShapeDtypeStruct((row_count, width), jnp.bfloat16)
    narrow_shape = jax.ShapeDtypeStruct((row_count, HEAD_DIM), jnp.bfloat16)
    sum_shape = jax.ShapeDtypeStruct((SLOT, HEAD_DIM), jnp.float32)
    flat_shape = jax.ShapeDtypeStruct((HEAD_DIM, SLOT), jnp.bfloat16)
    return pl.pallas_call(
        functools.partial(attend_kernel, len(heads), whole, len(held)),
        out_shape=(wide_shape,) * 2
        + ((narrow_shape,) * 2 if whole else (sum_shape,) * 2 + (flat_shape,) * 2),
        grid_spec=pltpu.PrefetchScalarGridSpec(
            num_scalar_prefetch=1,
            grid=(len(heads),),
            in_specs=in_specs,
            out_specs=(wide, wide, narrow, narrow) + (flat,) * 2 * (not whole),
            scratch_shapes=[pltpu.VMEM((HEAD_DIM, SLOT), jnp.bfloat16)] * 2 * whole
            + [pltpu.VMEM((SLOT, HEAD_DIM), jnp.float32)] * 2,
        ),
        input_output_aliases={1 + len(inputs) + i: i for i in range(len(held))},
        compiler_params=pltpu.CompilerParams(vmem_limit_bytes=16 * 1024 * 1024),
        cost_estimate=work(len(heads)),
        name="attend_" + "_".join(str(h) for h in heads),
    )(slot, *inputs, *held)


def product(a, b):
    return jnp.dot(a, b, preferred_element_type=jnp.float32)


def giver(made, places, sems):
    copies = [
        pltpu.make_async_copy(made.at[i], place, sems.at[i]) for i, place in enumerate(places)
    ]

    def give(i, value):
        made[i] = value.astype(jnp.bfloat16)
        copies[i].start()

    def settle():
        for copy in copies:
            copy.wait()

    return give, settle


def lanes(head):
    return pl.ds(head * HEAD_DIM, HEAD_DIM)


def part(ref, i):
    return ref[i * SLOT : (i + 1) * SLOT, :]


def middle_kernel(heads, blocks, slot_ref, most, mid, dk_in, dv_in, keys_t, values_t, *refs):
    o_ref, dq_ref, dk_ref, dv_ref, probs_ref, probs16_ref, made, sems = refs[2:]
    rows = pl.ds(pl.multiple_of(slot_ref[0] * SLOT, SLOT), SLOT)
    full, begun = heads
    places = (o_ref.at[rows, lanes(full)], dq_ref.at[rows, lanes(full)], o_ref.at[rows, lanes(begun)])
    give, settle = giver(made, places, sems)
    keys, values = part(most, blocks), part(most, blocks + 1)
    ids = numbers(most[(blocks + 2) * SLOT :, :])
    q, g = part(mid, 0), part(mid, 2)
    probs = attend_probs(ids, q, keys)
    probs16 = probs.astype(jnp.bfloat16)
    dscores = attend_dscores(probs, g, values)
    give(0, product(values_t[...], probs16).T)
    give(1, (product(keys_t[...], dscores) * SCALING).T)
    dv_ref[...] = dv_in[...] + product(probs16, g)
    dk_ref[...] = dk_in[...] + product(dscores, q)
    probs = attend_probs(ids, part(mid, 1), keys)
    probs16 = probs.astype(jnp.bfloat16)
    probs_ref[...] = probs
    probs16_ref[...] = probs16
    give(2, product(values_t[...], probs16).T)
    settle()


def finish_kernel(
    head, blocks, slot_ref, most, mid, last, dk_in, dv_in, probs_ref, probs16_ref, keys_t, *refs
):
    dq_ref, dk_ref, dv_ref, made, sems = refs[3:]
    rows = pl.ds(pl.multiple_of(slot_ref[0] * SLOT, SLOT), SLOT)
    places = (dq_ref.at[rows, lanes(head)], dk_ref.at[rows], dv_ref.at[rows])
    give, settle = giver(made, places, sems)
    q, g = part(mid, 1), last[...]
    dscores = attend_dscores(probs_ref[...], g, part(most, blocks + 1))
    give(2, dv_in[...] + product(probs16_ref[...], g))
    give(1, (dk_in[...] + product(dscores, q)) * SCALING)
    give(0, (product(keys_t[...], dscores) * SCALING).T)
    settle()


def one_step(kernel, name, slot, inputs, held, shapes, cost):
    vmem = pl.BlockSpec(memory_space=pltpu.VMEM)
    anywhere = pl.BlockSpec(memory_space=pl.ANY)
    return pl.pallas_call(
        kernel,
        out_shape=tuple(jax.ShapeDtypeStruct(x.shape, x.dtype) for x in held) + shapes,
        in_specs=[pl.BlockSpec(memory_space=pltpu.SMEM)]
        + [vmem] * len(inputs)
        + [anywhere] * len(held),
        out_specs=(anywhere,) * len(held) + (vmem,) * len(shapes),
        scratch_shapes=[
            pltpu.VMEM((3, SLOT, HEAD_DIM), jnp.bfloat16),
            pltpu.SemaphoreType.DMA((3,)),
        ],
        input_output_aliases={1 + len(inputs) + i: i for i in range(len(held))},
        compiler_params=pltpu.CompilerParams(vmem_limit_bytes=16 * 1024 * 1024),
        cost_estimate=work(cost),
        name=name,
    )(slot, *inputs, *held)


def body(query_rows, key_rows, value_rows, grad_rows, doc_ids, leaving_group):
    row_count, width = query_rows.shape
    heads = tuple(range(width // HEAD_DIM))
    early, late = heads[:-2], heads[-2:]
    group_count = row_count // SLOT
    far_bit = lax.axis_size("dp").bit_length() - 2

    most = pack(
        leaving_group, early, early, query_rows, grad_rows, (key_rows, value_rows), doc_ids
    )
    most, query_rows, grad_rows = lax.optimization_barrier((most, query_rows, grad_rows))
    most = swapped(most, "dp", far_bit)
    mid = pack(leaving_group, late, late[:1], query_rows, grad_rows)
    mid, query_rows, grad_rows = lax.optimization_barrier((mid, query_rows, grad_rows))
    mid = swapped(mid, "dp", far_bit)
    last = pack(leaving_group, (), late[1:], query_rows, grad_rows)
    last = swapped(last, "dp", far_bit)

    ids = jnp.pad(doc_ids.reshape(group_count, RUNS, LANES), ((0, 0), (0, 8 - RUNS), (0, 0)))
    marks = jnp.concatenate([ids // 16, ids % 16], axis=1).astype(jnp.bfloat16)
    staying = group_count - 1 - leaving_group

    held = attend(
        staying,
        heads,
        (
            marks.reshape(group_count * 16, LANES),
            *in_hbm((query_rows, grad_rows, key_rows, value_rows)),
        ),
        (
            lambda h, s: (s[0], 0),
            lambda h, s: (s[0], h),
            lambda h, s: (s[0], h),
            lambda h, s: (s[0], 0),
            lambda h, s: (s[0], 0),
        ),
        row_count,
        width,
    )

    pair_at = 2 * len(early)
    marks_at = (pair_at + 2) * (SLOT // 16)

    def marks_place(h, s):
        return (marks_at, 0)

    pair_places = (lambda h, s: (pair_at, 0), lambda h, s: (pair_at + 1, 0))
    out, dq, dk_sum, dv_sum, keys_t, values_t = attend(
        leaving_group,
        early,
        (most, most, most, most, most),
        (
            marks_place,
            lambda h, s: (h, 0),
            lambda h, s: (h + len(early), 0),
            *pair_places,
        ),
        row_count,
        width,
        held=held[:2],
    )
    sum_shape = jax.ShapeDtypeStruct((SLOT, HEAD_DIM), jnp.float32)
    square = [jax.ShapeDtypeStruct((SLOT, SLOT), t) for t in (jnp.float32, jnp.bfloat16)]
    out, dq, *sums = one_step(
        functools.partial(middle_kernel, late, pair_at),
        "middle",
        leaving_group,
        (most, mid, dk_sum, dv_sum, keys_t, values_t),
        (out, dq),
        (sum_shape, sum_shape, *square),
        2,
    )
    dq, dk, dv = one_step(
        functools.partial(finish_kernel, late[1], pair_at),
        "finish",
        leaving_group,
        (most, mid, last, *sums, keys_t),
        (dq, *held[2:]),
        (),
        1,
    )
    return out, dq, dk, dv


def solution(mesh):
    return jax.shard_map(
        body,
        mesh=mesh,
        in_specs=(P("dp", "mp"), P("dp", "mp"), P("dp", "mp"), P("dp", "mp"), P("dp"), P("dp")),
        out_specs=(P("dp", "mp"), P("dp", "mp"), P("dp", "mp"), P("dp", "mp")),
        check_vma=False,
    )
```

```python
import functools

import jax
import jax.numpy as jnp
from jax import lax
from jax.experimental import pallas as pl
from jax.experimental.pallas import tpu as pltpu
from jax.sharding import PartitionSpec as P

HEAD_DIM = 128
SLOT = 384
LANES = 128
RUNS = SLOT // LANES
LOG2E = 1.4426950408889634
SCALING = HEAD_DIM ** (-0.5)
MASKED = -1e30 * LOG2E
OVER_LANES = (((1,), (1,)), ((), ()))
RING = 16
YIELDING = (5, 7, 11, 13)
HBM = pl.BlockSpec(memory_space=pltpu.HBM)


def swapped(x, axis, bit):
    return lax.ppermute(x, axis, [(i, i ^ 1 << bit) for i in range(lax.axis_size(axis))])


def in_hbm(arrays):
    return [pltpu.with_memory_space_constraint(x, pltpu.HBM) for x in arrays]


def pack_kernel(q_heads, g_heads, whole, slot_ref, *refs):
    if whole:
        *inputs, ids_ref, out_ref, ids, sems = refs
        ids_copy = pltpu.make_async_copy(ids_ref, ids, sems.at[sems.shape[0] - 1])
        ids_copy.start()
    else:
        *inputs, out_ref, sems = refs
    rows = pl.ds(pl.multiple_of(slot_ref[0] * SLOT, SLOT), SLOT)
    parts = [
        ref.at[rows, pl.ds(h * HEAD_DIM, HEAD_DIM)]
        for ref, heads in zip(inputs, (q_heads, g_heads))
        for h in heads
    ]
    parts += [ref.at[rows] for ref in inputs[2:]]
    copies = [
        pltpu.make_async_copy(part, out_ref.at[pl.ds(i * SLOT, SLOT)], sems.at[i])
        for i, part in enumerate(parts)
    ]
    if whole:
        place = lax.axis_index("dp") * RING // lax.axis_size("dp")
        yields = functools.reduce(jnp.logical_or, [place == z for z in YIELDING])
        half = len(copies) // 2
        for copy in copies[:half]:
            copy.start()

        @pl.when(yields)
        def _():
            for copy in copies[:half]:
                copy.wait()

        for copy in copies[half:]:
            copy.start()
        ids_copy.wait()
        lines = [
            ids[j * LANES : (j + 1) * LANES].reshape(1, LANES) for j in range(ids.shape[0] // LANES)
        ]
        here = jnp.concatenate(lines[:RUNS], axis=0)
        for group in range(1, len(lines) // RUNS):
            other = jnp.concatenate(lines[group * RUNS : (group + 1) * RUNS], axis=0)
            here = jnp.where(slot_ref[0] == group, other, here)
        blank = jnp.zeros((8 - RUNS, LANES), jnp.int32)
        marks = jnp.concatenate([here >> 4, blank, here & 15, blank], axis=0)
        out_ref[len(parts) * SLOT :, :] = marks.astype(jnp.float32).astype(out_ref.dtype)

        @pl.when(jnp.logical_not(yields))
        def _():
            for copy in copies[:half]:
                copy.wait()

        for copy in copies[half:]:
            copy.wait()
    else:
        for copy in copies:
            copy.start()
        for copy in copies:
            copy.wait()


def pack(slot, q_heads, g_heads, query, grad, pair=(), doc_ids=None):
    whole = doc_ids is not None
    count = len(q_heads) + len(g_heads) + len(pair)
    inputs = (query, grad, *pair) + ((doc_ids,) if whole else ())
    inputs = in_hbm(inputs)
    packed = jax.ShapeDtypeStruct((count * SLOT + 16 * whole, HEAD_DIM), query.dtype)
    scratch = [pltpu.VMEM(doc_ids.shape, jnp.int32)] if whole else []
    return pl.pallas_call(
        functools.partial(pack_kernel, q_heads, g_heads, whole),
        out_shape=packed,
        in_specs=[pl.BlockSpec(memory_space=pltpu.SMEM)] + [HBM] * len(inputs),
        out_specs=pl.BlockSpec(memory_space=pltpu.VMEM),
        scratch_shapes=scratch + [pltpu.SemaphoreType.DMA((count + whole,))],
        compiler_params=pltpu.CompilerParams(vmem_limit_bytes=4 * 1024 * 1024),
        name=f"pack_{count}",
    )(slot, *inputs)


def attend_probs(ids, q, keys):
    scores = lax.dot_general(keys, q, OVER_LANES, preferred_element_type=jnp.float32)
    ids_t = ids.T
    key_ids = jnp.concatenate([ids_t[:, j : j + 1] for j in range(RUNS)], axis=0)
    row_ids = jnp.concatenate([ids[j : j + 1, :] for j in range(RUNS)], axis=1)
    key_places = lax.broadcasted_iota(jnp.int32, (SLOT, SLOT), 0)
    row_places = lax.broadcasted_iota(jnp.int32, (SLOT, SLOT), 1)
    allowed = (key_ids == row_ids) & (key_places <= row_places)
    scores = jnp.where(allowed, scores * (SCALING * LOG2E), MASKED)
    weights = jnp.exp2(scores - jnp.max(scores, axis=0, keepdims=True))
    return weights * (1.0 / jnp.sum(weights, axis=0, keepdims=True))


def attend_dscores(probs, g, values):
    dprobs = lax.dot_general(values, g, OVER_LANES, preferred_element_type=jnp.float32)
    inner_sum = jnp.sum(probs * dprobs, axis=0, keepdims=True)
    return (probs * (dprobs - inner_sum)).astype(jnp.bfloat16)


def attend_head(ids, q, g, keys, values, keys_t, values_t):
    probs = attend_probs(ids, q, keys)
    probs16 = probs.astype(jnp.bfloat16)
    dscores = attend_dscores(probs, g, values)
    dv = jnp.dot(probs16, g, preferred_element_type=jnp.float32)
    dk = jnp.dot(dscores, q, preferred_element_type=jnp.float32)
    out_t = jnp.dot(values_t, probs16, preferred_element_type=jnp.float32)
    dq_t = jnp.dot(keys_t, dscores, preferred_element_type=jnp.float32) * SCALING
    return out_t.T.astype(jnp.bfloat16), dq_t.T.astype(jnp.bfloat16), dk, dv


def numbers(marks):
    marks = marks.astype(jnp.float32)
    return marks[:8] * 16.0 + marks[8:]


def attend_kernel(count, slot_ref, marks_ref, q_ref, g_ref, k_ref, v_ref, *rest):
    o_ref, dq_ref, dk_ref, dv_ref, keys_t, values_t, dk_sum, dv_sum = rest
    index = pl.program_id(0)

    @pl.when(index == 0)
    def _():
        keys_t[...] = k_ref[...].T
        values_t[...] = v_ref[...].T
        dk_sum[...] = jnp.zeros_like(dk_sum)
        dv_sum[...] = jnp.zeros_like(dv_sum)

    ids = numbers(marks_ref[...])
    out, dq, dk, dv = attend_head(
        ids, q_ref[...], g_ref[...], k_ref[...], v_ref[...], keys_t[...], values_t[...]
    )
    o_ref[...] = out
    dq_ref[...] = dq
    dk_sum[...] += dk
    dv_sum[...] += dv

    @pl.when(index == count - 1)
    def _():
        dk_ref[...] = (dk_sum[...] * SCALING).astype(jnp.bfloat16)
        dv_ref[...] = dv_sum[...].astype(jnp.bfloat16)


def work(count):
    return pl.CostEstimate(
        flops=12 * count * SLOT * SLOT * HEAD_DIM,
        bytes_accessed=(4 * count + 4) * SLOT * HEAD_DIM * 2,
        transcendentals=SLOT * SLOT * count,
    )


def attend(slot, heads, inputs, places, row_count, width):
    def block(place, rows=SLOT):
        return pl.BlockSpec((rows, HEAD_DIM), place)

    wide = block(lambda h, s: (s[0], h))
    narrow = block(lambda h, s: (s[0], 0))
    wide_shape = jax.ShapeDtypeStruct((row_count, width), jnp.bfloat16)
    narrow_shape = jax.ShapeDtypeStruct((row_count, HEAD_DIM), jnp.bfloat16)
    return pl.pallas_call(
        functools.partial(attend_kernel, len(heads)),
        out_shape=(wide_shape,) * 2 + (narrow_shape,) * 2,
        grid_spec=pltpu.PrefetchScalarGridSpec(
            num_scalar_prefetch=1,
            grid=(len(heads),),
            in_specs=[block(places[0], 16)] + [block(place) for place in places[1:]],
            out_specs=(wide, wide, narrow, narrow),
            scratch_shapes=[pltpu.VMEM((HEAD_DIM, SLOT), jnp.bfloat16)] * 2
            + [pltpu.VMEM((SLOT, HEAD_DIM), jnp.float32)] * 2,
        ),
        compiler_params=pltpu.CompilerParams(vmem_limit_bytes=16 * 1024 * 1024),
        cost_estimate=work(len(heads)),
        name="attend_staying",
    )(slot, *inputs)


def product(a, b):
    return jnp.dot(a, b, preferred_element_type=jnp.float32)


def giver(made, places, sems):
    copies = [
        pltpu.make_async_copy(made.at[i], place, sems.at[i]) for i, place in enumerate(places)
    ]

    def give(i, value):
        made[i] = value.astype(jnp.bfloat16)
        copies[i].start()

    def settle():
        for copy in copies:
            copy.wait()

    return give, settle


def lanes(head):
    return pl.ds(head * HEAD_DIM, HEAD_DIM)


def part(ref, i):
    return ref[i * SLOT : (i + 1) * SLOT, :]


def early_kernel(heads, blocks, slot_ref, most, *refs):
    o_ref, dq_ref, dk_ref, dv_ref, keys_t, values_t, made, sems = refs[2:]
    rows = pl.ds(pl.multiple_of(slot_ref[0] * SLOT, SLOT), SLOT)
    places = [ref.at[rows, lanes(h)] for h in heads for ref in (o_ref, dq_ref)]
    give, settle = giver(made, places, sems)
    keys, values = part(most, blocks), part(most, blocks + 1)
    ids = numbers(most[(blocks + 2) * SLOT :, :])
    keys_t[...] = keys.T
    values_t[...] = values.T
    for i in range(len(heads)):
        q, g = part(most, i), part(most, len(heads) + i)
        probs = attend_probs(ids, q, keys)
        probs16 = probs.astype(jnp.bfloat16)
        dscores = attend_dscores(probs, g, values)
        give(2 * i, product(values_t[...], probs16).T)
        give(2 * i + 1, (product(keys_t[...], dscores) * SCALING).T)
        dv, dk = product(probs16, g), product(dscores, q)
        dv_ref[...] = dv if i == 0 else dv_ref[...] + dv
        dk_ref[...] = dk if i == 0 else dk_ref[...] + dk
    settle()


def finish_kernel(head, blocks, slot_ref, most, rest, dk_in, dv_in, keys_t, values_t, *refs):
    o_ref, dq_ref, dk_ref, dv_ref, made, sems = refs[4:]
    rows = pl.ds(pl.multiple_of(slot_ref[0] * SLOT, SLOT), SLOT)
    places = (o_ref.at[rows, lanes(head)], dq_ref.at[rows, lanes(head)])
    give, settle = giver(made, places + (dk_ref.at[rows], dv_ref.at[rows]), sems)
    ids = numbers(most[(blocks + 2) * SLOT :, :])
    q, g = part(rest, 0), part(rest, 1)
    probs = attend_probs(ids, q, part(most, blocks))
    probs16 = probs.astype(jnp.bfloat16)
    dscores = attend_dscores(probs, g, part(most, blocks + 1))
    give(3, dv_in[...] + product(probs16, g))
    give(0, product(values_t[...], probs16).T)
    give(2, (dk_in[...] + product(dscores, q)) * SCALING)
    give(1, (product(keys_t[...], dscores) * SCALING).T)
    settle()


def one_step(kernel, name, slot, inputs, held, shapes, copies, cost):
    vmem = pl.BlockSpec(memory_space=pltpu.VMEM)
    anywhere = pl.BlockSpec(memory_space=pl.ANY)
    return pl.pallas_call(
        kernel,
        out_shape=tuple(jax.ShapeDtypeStruct(x.shape, x.dtype) for x in held) + shapes,
        in_specs=[pl.BlockSpec(memory_space=pltpu.SMEM)]
        + [vmem] * len(inputs)
        + [anywhere] * len(held),
        out_specs=(anywhere,) * len(held) + (vmem,) * len(shapes),
        scratch_shapes=[
            pltpu.VMEM((copies, SLOT, HEAD_DIM), jnp.bfloat16),
            pltpu.SemaphoreType.DMA((copies,)),
        ],
        input_output_aliases={1 + len(inputs) + i: i for i in range(len(held))},
        compiler_params=pltpu.CompilerParams(vmem_limit_bytes=16 * 1024 * 1024),
        cost_estimate=work(cost),
        name=name,
    )(slot, *inputs, *held)


def body(query_rows, key_rows, value_rows, grad_rows, doc_ids, leaving_group):
    row_count, width = query_rows.shape
    heads = tuple(range(width // HEAD_DIM))
    early, late = heads[:-1], heads[-1:]
    group_count = row_count // SLOT
    far_bit = lax.axis_size("dp").bit_length() - 2

    most = pack(
        leaving_group, early, early, query_rows, grad_rows, (key_rows, value_rows), doc_ids
    )
    most, query_rows, grad_rows = lax.optimization_barrier((most, query_rows, grad_rows))
    most = swapped(most, "dp", far_bit)
    rest = pack(leaving_group, late, late, query_rows, grad_rows)
    rest = swapped(rest, "dp", far_bit)

    ids = jnp.pad(doc_ids.reshape(group_count, RUNS, LANES), ((0, 0), (0, 8 - RUNS), (0, 0)))
    marks = jnp.concatenate([ids // 16, ids % 16], axis=1).astype(jnp.bfloat16)
    staying = group_count - 1 - leaving_group

    held = attend(
        staying,
        heads,
        (
            marks.reshape(group_count * 16, LANES),
            *in_hbm((query_rows, grad_rows, key_rows, value_rows)),
        ),
        (
            lambda h, s: (s[0], 0),
            lambda h, s: (s[0], h),
            lambda h, s: (s[0], h),
            lambda h, s: (s[0], 0),
            lambda h, s: (s[0], 0),
        ),
        row_count,
        width,
    )

    pair_at = 2 * len(early)
    sum_shape = jax.ShapeDtypeStruct((SLOT, HEAD_DIM), jnp.float32)
    flat_shape = jax.ShapeDtypeStruct((HEAD_DIM, SLOT), jnp.bfloat16)
    out, dq, *sums = one_step(
        functools.partial(early_kernel, early, pair_at),
        "arrived_early",
        leaving_group,
        (most,),
        held[:2],
        (sum_shape, sum_shape, flat_shape, flat_shape),
        2 * len(early),
        len(early),
    )
    return one_step(
        functools.partial(finish_kernel, late[0], pair_at),
        "finish",
        leaving_group,
        (most, rest, *sums),
        (out, dq, *held[2:]),
        (),
        4,
        1,
    )


def solution(mesh):
    return jax.shard_map(
        body,
        mesh=mesh,
        in_specs=(P("dp", "mp"), P("dp", "mp"), P("dp", "mp"), P("dp", "mp"), P("dp"), P("dp")),
        out_specs=(P("dp", "mp"), P("dp", "mp"), P("dp", "mp"), P("dp", "mp")),
        check_vma=False,
    )
```

```python
import functools

import jax
import jax.numpy as jnp
from jax import lax
from jax.experimental import pallas as pl
from jax.experimental.pallas import tpu as pltpu
from jax.sharding import PartitionSpec as P

HEAD_DIM = 128
SLOT = 384
LANES = 128
RUNS = SLOT // LANES
LOG2E = 1.4426950408889634
SCALING = HEAD_DIM ** (-0.5)
MASKED = -1e30 * LOG2E
OVER_LANES = (((1,), (1,)), ((), ()))
RING = 16
YIELDING = (5, 7, 11, 13)
HBM = pl.BlockSpec(memory_space=pltpu.HBM)


def swapped(x, axis, bit):
    return lax.ppermute(x, axis, [(i, i ^ 1 << bit) for i in range(lax.axis_size(axis))])


def in_hbm(arrays):
    return [pltpu.with_memory_space_constraint(x, pltpu.HBM) for x in arrays]


def pack_kernel(q_heads, g_heads, whole, slot_ref, *refs):
    if whole:
        *inputs, ids_ref, out_ref, ids, sems = refs
        ids_copy = pltpu.make_async_copy(ids_ref, ids, sems.at[sems.shape[0] - 1])
        ids_copy.start()
    else:
        *inputs, out_ref, sems = refs
    rows = pl.ds(pl.multiple_of(slot_ref[0] * SLOT, SLOT), SLOT)
    parts = [
        ref.at[rows, pl.ds(h * HEAD_DIM, HEAD_DIM)]
        for ref, heads in zip(inputs, (q_heads, g_heads))
        for h in heads
    ]
    parts += [ref.at[rows] for ref in inputs[2:]]
    copies = [
        pltpu.make_async_copy(part, out_ref.at[pl.ds(i * SLOT, SLOT)], sems.at[i])
        for i, part in enumerate(parts)
    ]
    if whole:
        place = lax.axis_index("dp") * RING // lax.axis_size("dp")
        yields = functools.reduce(jnp.logical_or, [place == z for z in YIELDING])
        half = len(copies) // 2
        for copy in copies[:half]:
            copy.start()

        @pl.when(yields)
        def _():
            for copy in copies[:half]:
                copy.wait()

        for copy in copies[half:]:
            copy.start()
        ids_copy.wait()
        lines = [
            ids[j * LANES : (j + 1) * LANES].reshape(1, LANES) for j in range(ids.shape[0] // LANES)
        ]
        here = jnp.concatenate(lines[:RUNS], axis=0)
        for group in range(1, len(lines) // RUNS):
            other = jnp.concatenate(lines[group * RUNS : (group + 1) * RUNS], axis=0)
            here = jnp.where(slot_ref[0] == group, other, here)
        blank = jnp.zeros((8 - RUNS, LANES), jnp.int32)
        marks = jnp.concatenate([here >> 4, blank, here & 15, blank], axis=0)
        out_ref[len(parts) * SLOT :, :] = marks.astype(jnp.float32).astype(out_ref.dtype)

        @pl.when(jnp.logical_not(yields))
        def _():
            for copy in copies[:half]:
                copy.wait()

        for copy in copies[half:]:
            copy.wait()
    else:
        for copy in copies:
            copy.start()
        for copy in copies:
            copy.wait()


def pack(slot, q_heads, g_heads, query, grad, pair=(), doc_ids=None):
    whole = doc_ids is not None
    count = len(q_heads) + len(g_heads) + len(pair)
    inputs = (query, grad, *pair) + ((doc_ids,) if whole else ())
    inputs = in_hbm(inputs)
    packed = jax.ShapeDtypeStruct((count * SLOT + 16 * whole, HEAD_DIM), query.dtype)
    scratch = [pltpu.VMEM(doc_ids.shape, jnp.int32)] if whole else []
    return pl.pallas_call(
        functools.partial(pack_kernel, q_heads, g_heads, whole),
        out_shape=packed,
        in_specs=[pl.BlockSpec(memory_space=pltpu.SMEM)] + [HBM] * len(inputs),
        out_specs=pl.BlockSpec(memory_space=pltpu.VMEM),
        scratch_shapes=scratch + [pltpu.SemaphoreType.DMA((count + whole,))],
        compiler_params=pltpu.CompilerParams(vmem_limit_bytes=4 * 1024 * 1024),
        name=f"pack_{count}",
    )(slot, *inputs)


def allowed_of(ids):
    ids_t = ids.T
    key_ids = jnp.concatenate([ids_t[:, j : j + 1] for j in range(RUNS)], axis=0)
    row_ids = jnp.concatenate([ids[j : j + 1, :] for j in range(RUNS)], axis=1)
    key_places = lax.broadcasted_iota(jnp.int32, (SLOT, SLOT), 0)
    row_places = lax.broadcasted_iota(jnp.int32, (SLOT, SLOT), 1)
    return (key_ids == row_ids) & (key_places <= row_places)


def attend_probs(allowed, q, keys):
    scores = lax.dot_general(keys, q, OVER_LANES, preferred_element_type=jnp.float32)
    scores = jnp.where(allowed, scores * (SCALING * LOG2E), MASKED)
    weights = jnp.exp2(scores - jnp.max(scores, axis=0, keepdims=True))
    return weights * (1.0 / jnp.sum(weights, axis=0, keepdims=True))


def attend_dscores(probs, g, values):
    dprobs = lax.dot_general(values, g, OVER_LANES, preferred_element_type=jnp.float32)
    inner_sum = jnp.sum(probs * dprobs, axis=0, keepdims=True)
    return (probs * (dprobs - inner_sum)).astype(jnp.bfloat16)


def attend_head(ids, q, g, keys, values, keys_t, values_t):
    probs = attend_probs(allowed_of(ids), q, keys)
    probs16 = probs.astype(jnp.bfloat16)
    dscores = attend_dscores(probs, g, values)
    dv = jnp.dot(probs16, g, preferred_element_type=jnp.float32)
    dk = jnp.dot(dscores, q, preferred_element_type=jnp.float32)
    out_t = jnp.dot(values_t, probs16, preferred_element_type=jnp.float32)
    dq_t = jnp.dot(keys_t, dscores, preferred_element_type=jnp.float32) * SCALING
    return out_t.T.astype(jnp.bfloat16), dq_t.T.astype(jnp.bfloat16), dk, dv


def numbers(marks):
    marks = marks.astype(jnp.float32)
    return marks[:8] * 16.0 + marks[8:]


def attend_kernel(count, slot_ref, marks_ref, q_ref, g_ref, k_ref, v_ref, *rest):
    o_ref, dq_ref, dk_ref, dv_ref, keys_t, values_t, dk_sum, dv_sum = rest
    index = pl.program_id(0)

    @pl.when(index == 0)
    def _():
        keys_t[...] = k_ref[...].T
        values_t[...] = v_ref[...].T
        dk_sum[...] = jnp.zeros_like(dk_sum)
        dv_sum[...] = jnp.zeros_like(dv_sum)

    ids = numbers(marks_ref[...])
    out, dq, dk, dv = attend_head(
        ids, q_ref[...], g_ref[...], k_ref[...], v_ref[...], keys_t[...], values_t[...]
    )
    o_ref[...] = out
    dq_ref[...] = dq
    dk_sum[...] += dk
    dv_sum[...] += dv

    @pl.when(index == count - 1)
    def _():
        dk_ref[...] = (dk_sum[...] * SCALING).astype(jnp.bfloat16)
        dv_ref[...] = dv_sum[...].astype(jnp.bfloat16)


def work(count):
    return pl.CostEstimate(
        flops=12 * count * SLOT * SLOT * HEAD_DIM,
        bytes_accessed=(4 * count + 4) * SLOT * HEAD_DIM * 2,
        transcendentals=SLOT * SLOT * count,
    )


def attend(slot, heads, inputs, places, row_count, width):
    def block(place, rows=SLOT):
        return pl.BlockSpec((rows, HEAD_DIM), place)

    wide = block(lambda h, s: (s[0], h))
    narrow = block(lambda h, s: (s[0], 0))
    wide_shape = jax.ShapeDtypeStruct((row_count, width), jnp.bfloat16)
    narrow_shape = jax.ShapeDtypeStruct((row_count, HEAD_DIM), jnp.bfloat16)
    return pl.pallas_call(
        functools.partial(attend_kernel, len(heads)),
        out_shape=(wide_shape,) * 2 + (narrow_shape,) * 2,
        grid_spec=pltpu.PrefetchScalarGridSpec(
            num_scalar_prefetch=1,
            grid=(len(heads),),
            in_specs=[block(places[0], 16)] + [block(place) for place in places[1:]],
            out_specs=(wide, wide, narrow, narrow),
            scratch_shapes=[pltpu.VMEM((HEAD_DIM, SLOT), jnp.bfloat16)] * 2
            + [pltpu.VMEM((SLOT, HEAD_DIM), jnp.float32)] * 2,
        ),
        compiler_params=pltpu.CompilerParams(vmem_limit_bytes=16 * 1024 * 1024),
        cost_estimate=work(len(heads)),
        name="attend_staying",
    )(slot, *inputs)


def product(a, b):
    return jnp.dot(a, b, preferred_element_type=jnp.float32)


def giver(made, places, sems):
    copies = [
        pltpu.make_async_copy(made.at[i], place, sems.at[i]) for i, place in enumerate(places)
    ]

    def give(i, value):
        made[i] = value.astype(jnp.bfloat16)
        copies[i].start()

    def settle():
        for copy in copies:
            copy.wait()

    return give, settle


def lanes(head):
    return pl.ds(head * HEAD_DIM, HEAD_DIM)


def part(ref, i):
    return ref[i * SLOT : (i + 1) * SLOT, :]


def early_kernel(heads, blocks, slot_ref, most, *refs):
    o_ref, dq_ref, dk_ref, dv_ref, keys_t, values_t, mask, made, sems = refs[2:]
    rows = pl.ds(pl.multiple_of(slot_ref[0] * SLOT, SLOT), SLOT)
    places = [ref.at[rows, lanes(h)] for h in heads for ref in (o_ref, dq_ref)]
    give, settle = giver(made, places, sems)
    keys, values = part(most, blocks), part(most, blocks + 1)
    mask[...] = allowed_of(numbers(most[(blocks + 2) * SLOT :, :])).astype(jnp.float32)
    keys_t[...] = keys.T
    values_t[...] = values.T
    for i in range(len(heads)):
        q, g = part(most, i), part(most, len(heads) + i)
        probs = attend_probs(mask[...] > 0.5, q, keys)
        probs16 = probs.astype(jnp.bfloat16)
        dscores = attend_dscores(probs, g, values)
        give(2 * i, product(values_t[...], probs16).T)
        give(2 * i + 1, (product(keys_t[...], dscores) * SCALING).T)
        dv, dk = product(probs16, g), product(dscores, q)
        dv_ref[...] = dv if i == 0 else dv_ref[...] + dv
        dk_ref[...] = dk if i == 0 else dk_ref[...] + dk
    settle()


def finish_kernel(
    head, blocks, slot_ref, most, rest, dk_in, dv_in, keys_t, values_t, mask, *refs
):
    o_ref, dq_ref, dk_ref, dv_ref, made, sems = refs[4:]
    rows = pl.ds(pl.multiple_of(slot_ref[0] * SLOT, SLOT), SLOT)
    places = (o_ref.at[rows, lanes(head)], dq_ref.at[rows, lanes(head)])
    give, settle = giver(made, places + (dk_ref.at[rows], dv_ref.at[rows]), sems)
    q, g = part(rest, 0), part(rest, 1)
    probs = attend_probs(mask[...] > 0.5, q, part(most, blocks))
    probs16 = probs.astype(jnp.bfloat16)
    dscores = attend_dscores(probs, g, part(most, blocks + 1))
    give(3, dv_in[...] + product(probs16, g))
    give(0, product(values_t[...], probs16).T)
    give(2, (dk_in[...] + product(dscores, q)) * SCALING)
    give(1, (product(keys_t[...], dscores) * SCALING).T)
    settle()


def one_step(kernel, name, slot, inputs, held, shapes, copies, cost):
    vmem = pl.BlockSpec(memory_space=pltpu.VMEM)
    anywhere = pl.BlockSpec(memory_space=pl.ANY)
    return pl.pallas_call(
        kernel,
        out_shape=tuple(jax.ShapeDtypeStruct(x.shape, x.dtype) for x in held) + shapes,
        in_specs=[pl.BlockSpec(memory_space=pltpu.SMEM)]
        + [vmem] * len(inputs)
        + [anywhere] * len(held),
        out_specs=(anywhere,) * len(held) + (vmem,) * len(shapes),
        scratch_shapes=[
            pltpu.VMEM((copies, SLOT, HEAD_DIM), jnp.bfloat16),
            pltpu.SemaphoreType.DMA((copies,)),
        ],
        input_output_aliases={1 + len(inputs) + i: i for i in range(len(held))},
        compiler_params=pltpu.CompilerParams(vmem_limit_bytes=16 * 1024 * 1024),
        cost_estimate=work(cost),
        name=name,
    )(slot, *inputs, *held)


def body(query_rows, key_rows, value_rows, grad_rows, doc_ids, leaving_group):
    row_count, width = query_rows.shape
    heads = tuple(range(width // HEAD_DIM))
    early, late = heads[:-1], heads[-1:]
    group_count = row_count // SLOT
    far_bit = lax.axis_size("dp").bit_length() - 2

    most = pack(
        leaving_group, early, early, query_rows, grad_rows, (key_rows, value_rows), doc_ids
    )
    most, query_rows, grad_rows = lax.optimization_barrier((most, query_rows, grad_rows))
    most = swapped(most, "dp", far_bit)
    rest = pack(leaving_group, late, late, query_rows, grad_rows)
    rest = swapped(rest, "dp", far_bit)

    ids = jnp.pad(doc_ids.reshape(group_count, RUNS, LANES), ((0, 0), (0, 8 - RUNS), (0, 0)))
    marks = jnp.concatenate([ids // 16, ids % 16], axis=1).astype(jnp.bfloat16)
    staying = group_count - 1 - leaving_group

    held = attend(
        staying,
        heads,
        (
            marks.reshape(group_count * 16, LANES),
            *in_hbm((query_rows, grad_rows, key_rows, value_rows)),
        ),
        (
            lambda h, s: (s[0], 0),
            lambda h, s: (s[0], h),
            lambda h, s: (s[0], h),
            lambda h, s: (s[0], 0),
            lambda h, s: (s[0], 0),
        ),
        row_count,
        width,
    )

    pair_at = 2 * len(early)
    sum_shape = jax.ShapeDtypeStruct((SLOT, HEAD_DIM), jnp.float32)
    flat_shape = jax.ShapeDtypeStruct((HEAD_DIM, SLOT), jnp.bfloat16)
    square = jax.ShapeDtypeStruct((SLOT, SLOT), jnp.float32)
    out, dq, *sums = one_step(
        functools.partial(early_kernel, early, pair_at),
        "arrived_early",
        leaving_group,
        (most,),
        held[:2],
        (sum_shape, sum_shape, flat_shape, flat_shape, square),
        2 * len(early),
        len(early),
    )
    return one_step(
        functools.partial(finish_kernel, late[0], pair_at),
        "finish",
        leaving_group,
        (most, rest, *sums),
        (out, dq, *held[2:]),
        (),
        4,
        1,
    )


def solution(mesh):
    return jax.shard_map(
        body,
        mesh=mesh,
        in_specs=(P("dp", "mp"), P("dp", "mp"), P("dp", "mp"), P("dp", "mp"), P("dp"), P("dp")),
        out_specs=(P("dp", "mp"), P("dp", "mp"), P("dp", "mp"), P("dp", "mp")),
        check_vma=False,
    )
```

```python
import functools

import jax
import jax.numpy as jnp
from jax import lax
from jax.experimental import pallas as pl
from jax.experimental.pallas import tpu as pltpu
from jax.sharding import PartitionSpec as P

HEAD_DIM = 128
SLOT = 384
LANES = 128
RUNS = SLOT // LANES
LOG2E = 1.4426950408889634
SCALING = HEAD_DIM ** (-0.5)
MASKED = -1e30 * LOG2E
OVER_LANES = (((1,), (1,)), ((), ()))
RING = 16
YIELDING = (5, 7, 11, 13)
HBM = pl.BlockSpec(memory_space=pltpu.HBM)


def swapped(x, axis, bit):
    return lax.ppermute(x, axis, [(i, i ^ 1 << bit) for i in range(lax.axis_size(axis))])


def in_hbm(arrays):
    return [pltpu.with_memory_space_constraint(x, pltpu.HBM) for x in arrays]


def pack_kernel(q_heads, g_heads, whole, slot_ref, *refs):
    if whole:
        *inputs, ids_ref, out_ref, ids, sems = refs
        ids_copy = pltpu.make_async_copy(ids_ref, ids, sems.at[sems.shape[0] - 1])
        ids_copy.start()
    else:
        *inputs, out_ref, sems = refs
    rows = pl.ds(pl.multiple_of(slot_ref[0] * SLOT, SLOT), SLOT)
    parts = [
        ref.at[rows, pl.ds(h * HEAD_DIM, HEAD_DIM)]
        for ref, heads in zip(inputs, (q_heads, g_heads))
        for h in heads
    ]
    parts += [ref.at[rows] for ref in inputs[2:]]
    copies = [
        pltpu.make_async_copy(part, out_ref.at[pl.ds(i * SLOT, SLOT)], sems.at[i])
        for i, part in enumerate(parts)
    ]
    if whole:
        place = lax.axis_index("dp") * RING // lax.axis_size("dp")
        yields = functools.reduce(jnp.logical_or, [place == z for z in YIELDING])
        half = len(copies) // 2
        for copy in copies[:half]:
            copy.start()

        @pl.when(yields)
        def _():
            for copy in copies[:half]:
                copy.wait()

        for copy in copies[half:]:
            copy.start()
        ids_copy.wait()
        lines = [
            ids[j * LANES : (j + 1) * LANES].reshape(1, LANES) for j in range(ids.shape[0] // LANES)
        ]
        here = jnp.concatenate(lines[:RUNS], axis=0)
        for group in range(1, len(lines) // RUNS):
            other = jnp.concatenate(lines[group * RUNS : (group + 1) * RUNS], axis=0)
            here = jnp.where(slot_ref[0] == group, other, here)
        blank = jnp.zeros((8 - RUNS, LANES), jnp.int32)
        marks = jnp.concatenate([here >> 4, blank, here & 15, blank], axis=0)
        out_ref[len(parts) * SLOT :, :] = marks.astype(jnp.float32).astype(out_ref.dtype)

        @pl.when(jnp.logical_not(yields))
        def _():
            for copy in copies[:half]:
                copy.wait()

        for copy in copies[half:]:
            copy.wait()
    else:
        for copy in copies:
            copy.start()
        for copy in copies:
            copy.wait()


def pack(slot, q_heads, g_heads, query, grad, pair=(), doc_ids=None):
    whole = doc_ids is not None
    count = len(q_heads) + len(g_heads) + len(pair)
    inputs = (query, grad, *pair) + ((doc_ids,) if whole else ())
    inputs = in_hbm(inputs)
    packed = jax.ShapeDtypeStruct((count * SLOT + 16 * whole, HEAD_DIM), query.dtype)
    scratch = [pltpu.VMEM(doc_ids.shape, jnp.int32)] if whole else []
    return pl.pallas_call(
        functools.partial(pack_kernel, q_heads, g_heads, whole),
        out_shape=packed,
        in_specs=[pl.BlockSpec(memory_space=pltpu.SMEM)] + [HBM] * len(inputs),
        out_specs=pl.BlockSpec(memory_space=pltpu.VMEM),
        scratch_shapes=scratch + [pltpu.SemaphoreType.DMA((count + whole,))],
        compiler_params=pltpu.CompilerParams(vmem_limit_bytes=4 * 1024 * 1024),
        name=f"pack_{count}",
    )(slot, *inputs)


def allowed_of(ids):
    ids_t = ids.T
    key_ids = jnp.concatenate([ids_t[:, j : j + 1] for j in range(RUNS)], axis=0)
    row_ids = jnp.concatenate([ids[j : j + 1, :] for j in range(RUNS)], axis=1)
    key_places = lax.broadcasted_iota(jnp.int32, (SLOT, SLOT), 0)
    row_places = lax.broadcasted_iota(jnp.int32, (SLOT, SLOT), 1)
    return (key_ids == row_ids) & (key_places <= row_places)


def attend_probs(allowed, q, keys):
    scores = lax.dot_general(keys, q, OVER_LANES, preferred_element_type=jnp.float32)
    scores = jnp.where(allowed, scores * (SCALING * LOG2E), MASKED)
    weights = jnp.exp2(scores - jnp.max(scores, axis=0, keepdims=True))
    return weights * (1.0 / jnp.sum(weights, axis=0, keepdims=True))


def attend_dscores(probs, g, values):
    dprobs = lax.dot_general(values, g, OVER_LANES, preferred_element_type=jnp.float32)
    inner_sum = jnp.sum(probs * dprobs, axis=0, keepdims=True)
    return (probs * (dprobs - inner_sum)).astype(jnp.bfloat16)


def attend_head(ids, q, g, keys, values, keys_t, values_t):
    probs = attend_probs(allowed_of(ids), q, keys)
    probs16 = probs.astype(jnp.bfloat16)
    dscores = attend_dscores(probs, g, values)
    dv = jnp.dot(probs16, g, preferred_element_type=jnp.float32)
    dk = jnp.dot(dscores, q, preferred_element_type=jnp.float32)
    out_t = jnp.dot(values_t, probs16, preferred_element_type=jnp.float32)
    dq_t = jnp.dot(keys_t, dscores, preferred_element_type=jnp.float32) * SCALING
    return out_t.T.astype(jnp.bfloat16), dq_t.T.astype(jnp.bfloat16), dk, dv


def numbers(marks):
    marks = marks.astype(jnp.float32)
    return marks[:8] * 16.0 + marks[8:]


def attend_kernel(count, slot_ref, marks_ref, q_ref, g_ref, k_ref, v_ref, *rest):
    o_ref, dq_ref, dk_ref, dv_ref, keys_t, values_t, dk_sum, dv_sum = rest
    index = pl.program_id(0)

    @pl.when(index == 0)
    def _():
        keys_t[...] = k_ref[...].T
        values_t[...] = v_ref[...].T
        dk_sum[...] = jnp.zeros_like(dk_sum)
        dv_sum[...] = jnp.zeros_like(dv_sum)

    ids = numbers(marks_ref[...])
    out, dq, dk, dv = attend_head(
        ids, q_ref[...], g_ref[...], k_ref[...], v_ref[...], keys_t[...], values_t[...]
    )
    o_ref[...] = out
    dq_ref[...] = dq
    dk_sum[...] += dk
    dv_sum[...] += dv

    @pl.when(index == count - 1)
    def _():
        dk_ref[...] = (dk_sum[...] * SCALING).astype(jnp.bfloat16)
        dv_ref[...] = dv_sum[...].astype(jnp.bfloat16)


def work(count):
    return pl.CostEstimate(
        flops=12 * count * SLOT * SLOT * HEAD_DIM,
        bytes_accessed=(4 * count + 4) * SLOT * HEAD_DIM * 2,
        transcendentals=SLOT * SLOT * count,
    )


def attend(slot, heads, inputs, places, row_count, width):
    def block(place, rows=SLOT):
        return pl.BlockSpec((rows, HEAD_DIM), place)

    wide = block(lambda h, s: (s[0], h))
    narrow = block(lambda h, s: (s[0], 0))
    wide_shape = jax.ShapeDtypeStruct((row_count, width), jnp.bfloat16)
    narrow_shape = jax.ShapeDtypeStruct((row_count, HEAD_DIM), jnp.bfloat16)
    return pl.pallas_call(
        functools.partial(attend_kernel, len(heads)),
        out_shape=(wide_shape,) * 2 + (narrow_shape,) * 2,
        grid_spec=pltpu.PrefetchScalarGridSpec(
            num_scalar_prefetch=1,
            grid=(len(heads),),
            in_specs=[block(places[0], 16)] + [block(place) for place in places[1:]],
            out_specs=(wide, wide, narrow, narrow),
            scratch_shapes=[pltpu.VMEM((HEAD_DIM, SLOT), jnp.bfloat16)] * 2
            + [pltpu.VMEM((SLOT, HEAD_DIM), jnp.float32)] * 2,
        ),
        compiler_params=pltpu.CompilerParams(vmem_limit_bytes=16 * 1024 * 1024),
        cost_estimate=work(len(heads)),
        name="attend_staying",
    )(slot, *inputs)


def product(a, b):
    return jnp.dot(a, b, preferred_element_type=jnp.float32)


def giver(made, places, sems):
    copies = [
        pltpu.make_async_copy(made.at[i], place, sems.at[i]) for i, place in enumerate(places)
    ]

    def give(i, value):
        made[i] = value.astype(jnp.bfloat16)
        copies[i].start()

    def settle():
        for copy in copies:
            copy.wait()

    return give, settle


def lanes(head):
    return pl.ds(head * HEAD_DIM, HEAD_DIM)


def part(ref, i):
    return ref[i * SLOT : (i + 1) * SLOT, :]


def early_kernel(heads, blocks, slot_ref, most, *refs):
    o_ref, dq_ref, dk_ref, dv_ref, keys_t, values_t, mask, made, sems = refs[2:]
    rows = pl.ds(pl.multiple_of(slot_ref[0] * SLOT, SLOT), SLOT)
    places = [ref.at[rows, lanes(h)] for h in heads for ref in (o_ref, dq_ref)]
    give, settle = giver(made, places, sems)
    keys, values = part(most, blocks), part(most, blocks + 1)
    mask[...] = allowed_of(numbers(most[(blocks + 2) * SLOT :, :])).astype(jnp.float32)
    keys_t[...] = keys.T
    values_t[...] = values.T
    for i in range(len(heads)):
        q, g = part(most, i), part(most, len(heads) + i)
        probs = attend_probs(mask[...] > 0.5, q, keys)
        probs16 = probs.astype(jnp.bfloat16)
        dscores = attend_dscores(probs, g, values)
        give(2 * i, product(values_t[...], probs16).T)
        give(2 * i + 1, (product(keys_t[...], dscores) * SCALING).T)
        dv, dk = product(probs16, g), product(dscores, q)
        dv_ref[...] = dv if i == 0 else dv_ref[...] + dv
        dk_ref[...] = dk if i == 0 else dk_ref[...] + dk
    settle()


def finish_kernel(
    head, blocks, slot_ref, most, rest, dk_in, dv_in, keys_t, values_t, mask, *refs
):
    o_ref, dq_ref, dk_ref, dv_ref, made, sems = refs[4:]
    rows = pl.ds(pl.multiple_of(slot_ref[0] * SLOT, SLOT), SLOT)
    places = (o_ref.at[rows, lanes(head)], dq_ref.at[rows, lanes(head)])
    give, settle = giver(made, places + (dk_ref.at[rows], dv_ref.at[rows]), sems)
    q, g = part(rest, 0), part(rest, 1)
    probs = attend_probs(mask[...] > 0.5, q, part(most, blocks))
    probs16 = probs.astype(jnp.bfloat16)
    dscores = attend_dscores(probs, g, part(most, blocks + 1))
    give(3, dv_in[...] + product(probs16, g))
    give(0, product(values_t[...], probs16).T)
    give(1, (product(keys_t[...], dscores) * SCALING).T)
    give(2, (dk_in[...] + product(dscores, q)) * SCALING)
    settle()


def one_step(kernel, name, slot, inputs, held, shapes, copies, cost):
    vmem = pl.BlockSpec(memory_space=pltpu.VMEM)
    anywhere = pl.BlockSpec(memory_space=pl.ANY)
    return pl.pallas_call(
        kernel,
        out_shape=tuple(jax.ShapeDtypeStruct(x.shape, x.dtype) for x in held) + shapes,
        in_specs=[pl.BlockSpec(memory_space=pltpu.SMEM)]
        + [vmem] * len(inputs)
        + [anywhere] * len(held),
        out_specs=(anywhere,) * len(held) + (vmem,) * len(shapes),
        scratch_shapes=[
            pltpu.VMEM((copies, SLOT, HEAD_DIM), jnp.bfloat16),
            pltpu.SemaphoreType.DMA((copies,)),
        ],
        input_output_aliases={1 + len(inputs) + i: i for i in range(len(held))},
        compiler_params=pltpu.CompilerParams(vmem_limit_bytes=16 * 1024 * 1024),
        cost_estimate=work(cost),
        name=name,
    )(slot, *inputs, *held)


def body(query_rows, key_rows, value_rows, grad_rows, doc_ids, leaving_group):
    row_count, width = query_rows.shape
    heads = tuple(range(width // HEAD_DIM))
    early, late = heads[:-1], heads[-1:]
    group_count = row_count // SLOT
    far_bit = lax.axis_size("dp").bit_length() - 2

    most = pack(
        leaving_group, early, early, query_rows, grad_rows, (key_rows, value_rows), doc_ids
    )
    most, query_rows, grad_rows = lax.optimization_barrier((most, query_rows, grad_rows))
    most = swapped(most, "dp", far_bit)
    rest = pack(leaving_group, late, late, query_rows, grad_rows)
    rest = swapped(rest, "dp", far_bit)

    ids = jnp.pad(doc_ids.reshape(group_count, RUNS, LANES), ((0, 0), (0, 8 - RUNS), (0, 0)))
    marks = jnp.concatenate([ids // 16, ids % 16], axis=1).astype(jnp.bfloat16)
    staying = group_count - 1 - leaving_group

    held = attend(
        staying,
        heads,
        (
            marks.reshape(group_count * 16, LANES),
            *in_hbm((query_rows, grad_rows, key_rows, value_rows)),
        ),
        (
            lambda h, s: (s[0], 0),
            lambda h, s: (s[0], h),
            lambda h, s: (s[0], h),
            lambda h, s: (s[0], 0),
            lambda h, s: (s[0], 0),
        ),
        row_count,
        width,
    )

    pair_at = 2 * len(early)
    sum_shape = jax.ShapeDtypeStruct((SLOT, HEAD_DIM), jnp.float32)
    flat_shape = jax.ShapeDtypeStruct((HEAD_DIM, SLOT), jnp.bfloat16)
    square = jax.ShapeDtypeStruct((SLOT, SLOT), jnp.float32)
    out, dq, *sums = one_step(
        functools.partial(early_kernel, early, pair_at),
        "arrived_early",
        leaving_group,
        (most,),
        held[:2],
        (sum_shape, sum_shape, flat_shape, flat_shape, square),
        2 * len(early),
        len(early),
    )
    return one_step(
        functools.partial(finish_kernel, late[0], pair_at),
        "finish",
        leaving_group,
        (most, rest, *sums),
        (out, dq, *held[2:]),
        (),
        4,
        1,
    )


def solution(mesh):
    return jax.shard_map(
        body,
        mesh=mesh,
        in_specs=(P("dp", "mp"), P("dp", "mp"), P("dp", "mp"), P("dp", "mp"), P("dp"), P("dp")),
        out_specs=(P("dp", "mp"), P("dp", "mp"), P("dp", "mp"), P("dp", "mp")),
        check_vma=False,
    )
```
